256 devices in a mesh: leaf: 32 (over z, x), panel: 8 (over y, core).
Axes of the slice: x: 4, y: 4, z: 8, core: 2. Of those that a mesh axis runs over, the one named last changes fastest.
Arguments:
- leaf_sides: bfloat16 [65536, 128], P(('leaf', 'panel')), may hold values from -6 to 6
- leaf_inverse: bfloat16 [65536, 2048], P(('leaf', 'panel')), may hold values from -0.1875 to 0.1875
- leaf_panels: bfloat16 [3, 4096, 65536], P(None, 'panel', 'leaf'), may hold values from -0.125 to 0.125
- parent_map: int32 [32], P('leaf'), may hold values from 0 to 3, as said below
- tile_mask: int32 [32, 3, 32], P('leaf'), may hold values 0 or 1
- top_sides: bfloat16 [7, 4096, 128], P(None, ('panel', 'leaf')), may hold values from -6 to 6
- grand_inverse: bfloat16 [16384, 4096], P('leaf', 'panel'), may hold values from -0.125 to 0.125
- child_inverse: bfloat16 [8192, 4096], P('leaf', 'panel'), may hold values from -0.125 to 0.125
- root_inverse: bfloat16 [4096, 4096], P('leaf', 'panel'), may hold values from -0.125 to 0.125
- child_panels: bfloat16 [4096, 16384], P('panel', 'leaf'), may hold values from -0.09375 to 0.09375
- root_grand: bfloat16 [4096, 16384], P('panel', 'leaf'), may hold values from -0.09375 to 0.09375
- root_child: bfloat16 [4096, 8192], P('panel', 'leaf'), may hold values from -0.09375 to 0.09375
Outputs:
- leaf_solution: bfloat16 [65536, 128], P(('leaf', 'panel'))
- top_solution: bfloat16 [7, 4096, 128], P(None, ('panel', 'leaf'))
The draws below stay inside these ranges and needn't reach their ends.
Inputs may be any that keep to these rules, and one draw needn't show every extreme that they name: `parent_map`: each of the 4 grandchild separators is the parent of at least one subtree.
All inputs are finite; a program needn't handle non-finite values. No bound on the sum of `tile_mask` on one device may be relied on, other than what follows from the above.
Results may differ from the reference program's by a relative error of at most 0.017.
Values may be sent and summed in bfloat16 or wider, within the bound.
A program may use at most 64 MiB of HBM per device.

```python
import jax
import jax.numpy as jnp
from jax import lax

S = 4096
W = 2048
R = 128
TILE_ROWS = 128
SUBTREES = 32


def draw_parent_map(key, part):
    key_labels = jax.random.fold_in(key, 101)
    key_first = jax.random.fold_in(key, 202)
    key_second = jax.random.fold_in(key, 303)
    key_order = jax.random.fold_in(key, 404)
    labels = jax.random.permutation(key_labels, jnp.arange(4, dtype=jnp.int32))
    first_pick = jax.random.randint(key_first, (SUBTREES,), 0, 4, dtype=jnp.int32)
    second_pick = jax.random.randint(key_second, (SUBTREES,), 0, 4, dtype=jnp.int32)
    ranked = jnp.minimum(first_pick, second_pick)
    ranked = ranked.at[0:4].set(jnp.arange(4, dtype=jnp.int32))
    shuffled = jax.random.permutation(key_order, jnp.arange(SUBTREES, dtype=jnp.int32))
    return labels[ranked[shuffled]].astype(jnp.int32)


def set_ends(result, own_key, least, largest):
    longest = result.shape.index(max(result.shape))
    spots = []
    for shift in (0, 1):
        where = [jax.random.randint(jax.random.fold_in(own_key, axis), (), 0, length) for axis, length in enumerate(result.shape)]
        where[longest] = (where[longest] + shift) % result.shape[longest]
        spots.append(tuple(where))
    return result.at[spots[0]].set(least).at[spots[1]].set(largest)


def steps_of(rng, dims, shards, low, top_value):
    def one(axis_at, shards_of):
        heights = jax.random.uniform(jax.random.fold_in(jax.random.fold_in(rng, 6), axis_at), (shards_of,), jnp.float32, low / len(shards), top_value / len(shards))
        return jnp.repeat(jnp.exp(heights), dims[axis_at] // shards_of).reshape((-1,) + (1,) * (len(dims) - axis_at - 1))

    gain = one(*shards[0])
    for cut in shards[1:]:
        gain = gain * one(*cut)
    return gain


def normal_values(own_key, extent, deviation, limit, pieces=(), held_as=jnp.bfloat16):
    result = deviation * jax.random.normal(own_key, extent, jnp.float32)
    if pieces:
        result = result * steps_of(own_key, extent, pieces, -0.22, 0.18)
    return jnp.clip(result, -limit, limit).astype(held_as)


def setup_inputs(seed: int = 0) -> dict:
    splits = jax.random.split(jax.random.key(seed), 13)
    return {
        "leaf_sides": normal_values(splits[0], (SUBTREES * W, R), 1.0, 6.0, ((0, 256),)),
        "leaf_inverse": normal_values(splits[1], (SUBTREES * W, W), (W // 2) ** -0.5, 0.1875, ((0, 256),)),
        "leaf_panels": normal_values(splits[2], (3, S, SUBTREES * W), W ** -0.5, 0.125, ((1, 8), (2, 32))),
        "parent_map": draw_parent_map(jax.random.fold_in(splits[12], 71), 0),
        "tile_mask": set_ends((jax.random.randint(splits[4], (SUBTREES, 3, S // TILE_ROWS), 0, 2) < 1).astype(jnp.int32), jax.random.fold_in(splits[4], 1), 0, 1),
        "top_sides": normal_values(splits[5], (7, S, R), 1.0, 6.0, ((1, 256),)),
        "grand_inverse": normal_values(splits[6], (4 * S, S), (S // 2) ** -0.5, 0.125, ((0, 32), (1, 8))),
        "child_inverse": normal_values(splits[7], (2 * S, S), (S // 2) ** -0.5, 0.125, ((0, 32), (1, 8))),
        "root_inverse": normal_values(splits[8], (S, S), (S // 2) ** -0.5, 0.125, ((0, 32), (1, 8))),
        "child_panels": normal_values(splits[9], (S, 4 * S), S ** -0.5, 0.09375, ((0, 8), (1, 32))),
        "root_grand": normal_values(splits[10], (S, 4 * S), S ** -0.5, 0.09375, ((0, 8), (1, 32))),
        "root_child": normal_values(splits[11], (S, 2 * S), S ** -0.5, 0.09375, ((0, 8), (1, 32))),
    }


def lower_block(matrix, first_row, count):
    return jnp.tril(lax.dynamic_slice_in_dim(matrix, first_row, count, 0))


def reference(leaf_sides, leaf_inverse, leaf_panels, parent_map, tile_mask, top_sides, grand_inverse, child_inverse, root_inverse, child_panels, root_grand, root_child):
    subtrees = parent_map.shape[0]
    leaf_width = leaf_inverse.shape[1]
    separator = root_inverse.shape[0]
    side_count = leaf_sides.shape[1]
    subtree_list = jnp.arange(subtrees, dtype=jnp.int32)

    def expand_mask(subtree):
        tile_flags = lax.dynamic_index_in_dim(tile_mask, subtree, 0, keepdims=False).astype(jnp.float32)
        return jnp.repeat(tile_flags, TILE_ROWS, axis=1)

    def forward(running, subtree):
        first_row = subtree * leaf_width
        right_sides = lax.dynamic_slice_in_dim(leaf_sides, first_row, leaf_width, 0)
        triangle = lower_block(leaf_inverse, first_row, leaf_width)
        solved = jnp.dot(triangle, right_sides, preferred_element_type=jnp.float32).astype(jnp.bfloat16)
        panels = lax.dynamic_slice_in_dim(leaf_panels, first_row, leaf_width, 2)
        updates = jnp.stack([jnp.dot(panels[ancestor], solved, preferred_element_type=jnp.float32) for ancestor in range(3)])
        updates = updates * expand_mask(subtree)[:, :, None]
        parent = lax.dynamic_index_in_dim(parent_map, subtree, 0, keepdims=False)
        grand_slots = (jnp.arange(4, dtype=jnp.int32) == parent).astype(jnp.float32)
        child_slots = (jnp.arange(2, dtype=jnp.int32) == parent // 2).astype(jnp.float32)
        grand_sum, child_sum, root_sum = running
        return (grand_sum + grand_slots[:, None, None] * updates[0][None], child_sum + child_slots[:, None, None] * updates[1][None], root_sum + updates[2]), solved

    initial = (jnp.zeros((4, separator, side_count), jnp.float32), jnp.zeros((2, separator, side_count), jnp.float32), jnp.zeros((separator, side_count), jnp.float32))
    (grand_leaf, child_leaf, root_leaf), leaf_solved = lax.scan(forward, initial, subtree_list)

    top_right = top_sides.astype(jnp.float32)
    grand_lower = [jnp.tril(grand_inverse[slot * separator:(slot + 1) * separator]) for slot in range(4)]
    child_lower = [jnp.tril(child_inverse[slot * separator:(slot + 1) * separator]) for slot in range(2)]
    root_lower = jnp.tril(root_inverse)

    grand_solved = []
    for slot in range(4):
        grand_right = (top_right[slot] - grand_leaf[slot]).astype(jnp.bfloat16)
        grand_solved.append(jnp.dot(grand_lower[slot], grand_right, preferred_element_type=jnp.float32).astype(jnp.bfloat16))
    child_solved = []
    for slot in range(2):
        child_right = top_right[4 + slot] - child_leaf[slot]
        for grand_slot in (2 * slot, 2 * slot + 1):
            child_right = child_right - jnp.dot(child_panels[:, grand_slot * separator:(grand_slot + 1) * separator], grand_solved[grand_slot], preferred_element_type=jnp.float32)
        child_solved.append(jnp.dot(child_lower[slot], child_right.astype(jnp.bfloat16), preferred_element_type=jnp.float32).astype(jnp.bfloat16))
    root_right = top_right[6] - root_leaf
    for slot in range(4):
        root_right = root_right - jnp.dot(root_grand[:, slot * separator:(slot + 1) * separator], grand_solved[slot], preferred_element_type=jnp.float32)
    for slot in range(2):
        root_right = root_right - jnp.dot(root_child[:, slot * separator:(slot + 1) * separator], child_solved[slot], preferred_element_type=jnp.float32)
    root_solved = jnp.dot(root_lower, root_right.astype(jnp.bfloat16), preferred_element_type=jnp.float32).astype(jnp.bfloat16)

    root_result = jnp.dot(root_lower.T, root_solved, preferred_element_type=jnp.float32).astype(jnp.bfloat16)
    child_result = []
    for slot in range(2):
        residual = child_solved[slot].astype(jnp.float32) - jnp.dot(root_child[:, slot * separator:(slot + 1) * separator].T, root_result, preferred_element_type=jnp.float32)
        child_result.append(jnp.dot(child_lower[slot].T, residual.astype(jnp.bfloat16), preferred_element_type=jnp.float32).astype(jnp.bfloat16))
    grand_result = []
    for slot in range(4):
        residual = grand_solved[slot].astype(jnp.float32)
        residual = residual - jnp.dot(child_panels[:, slot * separator:(slot + 1) * separator].T, child_result[slot // 2], preferred_element_type=jnp.float32)
        residual = residual - jnp.dot(root_grand[:, slot * separator:(slot + 1) * separator].T, root_result, preferred_element_type=jnp.float32)
        grand_result.append(jnp.dot(grand_lower[slot].T, residual.astype(jnp.bfloat16), preferred_element_type=jnp.float32).astype(jnp.bfloat16))
    grand_stack = jnp.stack(grand_result)
    child_stack = jnp.stack(child_result)

    def backward(running, subtree):
        first_row = subtree * leaf_width
        parent = lax.dynamic_index_in_dim(parent_map, subtree, 0, keepdims=False)
        ancestors = jnp.stack([lax.dynamic_index_in_dim(grand_stack, parent, 0, keepdims=False), lax.dynamic_index_in_dim(child_stack, parent // 2, 0, keepdims=False), root_result])
        ancestors = ancestors * expand_mask(subtree)[:, :, None].astype(jnp.bfloat16)
        panels = lax.dynamic_slice_in_dim(leaf_panels, first_row, leaf_width, 2)
        pulled = sum([jnp.dot(panels[ancestor].T, ancestors[ancestor], preferred_element_type=jnp.float32) for ancestor in range(3)])
        solved = lax.dynamic_index_in_dim(leaf_solved, subtree, 0, keepdims=False)
        residual = (solved.astype(jnp.float32) - pulled).astype(jnp.bfloat16)
        triangle = lower_block(leaf_inverse, first_row, leaf_width)
        return running, jnp.dot(triangle.T, residual, preferred_element_type=jnp.float32).astype(jnp.bfloat16)

    unused, leaf_result = lax.scan(backward, jnp.zeros((), jnp.float32), subtree_list)
    leaf_solution = leaf_result.reshape(subtrees * leaf_width, side_count)
    top_solution = jnp.concatenate([grand_stack, child_stack, root_result[None]], axis=0)
    return leaf_solution, top_solution
```

```python
import functools

import jax
import jax.numpy as jnp
from jax import lax
from jax.experimental import pallas as pl
from jax.experimental.pallas import tpu as pltpu
from jax.sharding import PartitionSpec as P

MESH = pl.DeviceIdType.MESH
F32 = jnp.float32
BF16 = jnp.bfloat16
LEAF = 32
PANEL = 8

(X_SIDES, X_WEIGHT, X_SOLVED, X_U0, X_U12, X_GRIGHT, X_GRED, X_GSOL, X_CTOP, X_CRED, X_CRIGHT, X_CRED2, X_CSOL,
 X_RRED, X_RRIGHT, X_RRED2, X_RSOL, X_RBACK, X_RRES, X_CBACK, X_CRESID, X_CBACK2, X_CRES, X_CFAR, X_GBACK, X_GRESID,
 X_GBACK2, X_GRES, X_PULL, X_OUT, X_COUNT) = range(31)


def lower_mask(ref, out, row0, col0, tile):
    rows, cols = ref.shape

    def body(i, c):
        at = pl.ds(pl.multiple_of(i * tile, tile), tile)
        row = row0 + i * tile + lax.broadcasted_iota(jnp.int32, (tile, cols), 0)
        col = col0 + lax.broadcasted_iota(jnp.int32, (tile, cols), 1)
        out[at, :] = jnp.where(row >= col, ref[at, :].astype(F32), 0.0).astype(BF16)
        return c

    lax.fori_loop(0, rows // tile, body, 0)


def dot(a, b):
    return jnp.dot(a, b, preferred_element_type=F32)


def dot_t(a, b):
    return lax.dot_general(a, b, (((0,), (0,)), ((), ())), preferred_element_type=F32)


def kernel(
    parent, tiles, sides, inverse_h, panels_h, tops, grand_h, child_h, root_h, cp_h, rg_h, rc_h,
    leaf_out, top_out,
    inverse, panels, grand, child, root, cp, rg, rc,
    in_sem, send_sem, recv_sem,
    sides_all, weight, solved_all, u0_out, u12_out, u0_in, u12_in,
    gright_out, gright, gred_out, gred, gsol, ctop_out, ctop, cred_out, cred, cright, cred2_out, cred2, csol,
    rred_out, rred, rright, rred2_out, rred2, rsol, rback_out, rback, rres, cback_out, cback, cresid,
    cback2_out, cback2, cres, cfar, gback_out, gback, gresid, gback2_out, gback2, gres,
    pulled, pull_out, pull, leafo_out, leafo, ancestor, rg_part, gb_part,
):
    l = lax.axis_index("leaf")
    p = lax.axis_index("panel")
    l8, l16 = l // 8 * 8, l // 16 * 16
    m8, m16 = l - l8, l - l16

    loads = []
    for i, (src, dst) in enumerate(
        [(inverse_h, inverse), (panels_h, panels), (grand_h, grand), (cp_h, cp), (rg_h, rg), (child_h, child), (rc_h, rc), (root_h, root)]
    ):
        copy = pltpu.make_async_copy(src, dst, in_sem.at[i])
        copy.start()
        loads.append(copy)

    barrier = pltpu.get_barrier_semaphore()

    def greet_leaf(k, c):
        pl.semaphore_signal(barrier, inc=1, device_id=(lax.rem(l + k, LEAF), p), device_id_type=MESH)
        return c

    def greet_panel(k, c):
        pl.semaphore_signal(barrier, inc=1, device_id=(l, lax.rem(p + k, PANEL)), device_id_type=MESH)
        return c

    lax.fori_loop(1, PANEL, greet_panel, 0)
    lax.fori_loop(1, LEAF, greet_leaf, 0)

    def send(x, src, dst, device):
        pltpu.make_async_remote_copy(src, dst, send_sem.at[x], recv_sem.at[x], device_id=device, device_id_type=MESH).start()

    def arrived(x, ref):
        pltpu.make_async_copy(ref, ref, recv_sem.at[x]).wait()

    def to_panel(x, src_of, dst):
        def body(k, c):
            q = lax.rem(p + k, PANEL)
            send(x, src_of(q), dst, (l, q))
            return c

        lax.fori_loop(1, PANEL, body, 0)

    def to_leaf(x, n, base, me, src_of, dst):
        def body(k, c):
            q = lax.rem(me + k, n)
            send(x, src_of(q), dst, (base + q, p))
            return c

        lax.fori_loop(n // 2, n, body, 0)
        lax.fori_loop(1, n // 2, body, 0)

    def total(ref):
        return jnp.sum(ref[...].astype(F32), axis=0)

    def flat(ref):
        return ref[...].reshape(ref.shape[0] * ref.shape[1], ref.shape[2])

    def scattered(value, out):
        out[...] = value.astype(BF16).reshape(out.shape)

    mine = parent[0]
    own_grand = [jnp.where(mine == g, 1.0, 0.0).astype(F32) for g in range(4)]
    own_child = [own_grand[0] + own_grand[1], own_grand[2] + own_grand[3]]
    slot = lax.broadcasted_iota(jnp.int32, (16, 128), 0)
    picks = jnp.zeros((16, 128), F32)
    for g in range(4):
        picks = picks + jnp.where(slot == g, own_grand[g], 0.0)
    for c in range(2):
        picks = picks + jnp.where(slot == 4 + c, own_child[c], 0.0)
    weight[l] = picks.astype(BF16)
    sides_all[p] = sides[...]

    pl.semaphore_wait(barrier, LEAF - 1 + PANEL - 1)

    to_panel(X_SIDES, lambda q: sides_all.at[p], sides_all.at[p])
    to_leaf(X_WEIGHT, LEAF, 0, l, lambda q: weight.at[l], weight.at[l])
    loads[0].wait()
    lower_mask(inverse, inverse, p * 256, 0, 32)
    arrived(X_SIDES, sides_all.at[pl.ds(0, PANEL - 1)])
    solved_all[p] = dot(inverse[...], flat(sides_all)).astype(BF16)
    to_panel(X_SOLVED, lambda q: solved_all.at[p], solved_all.at[p])
    loads[1].wait()
    loads[2].wait()
    lower_mask(grand, grand, m8 * 512, p * 512, 64)
    loads[5].wait()
    lower_mask(child, child, m16 * 256, p * 512, 64)
    loads[7].wait()
    lower_mask(root, root, l * 128, p * 512, 64)
    arrived(X_SOLVED, solved_all.at[pl.ds(0, PANEL - 1)])

    def update(k):
        for t in range(4):
            keep = tiles[0, k, p * 4 + t].astype(F32)
            value = dot(panels[k, t * 128:(t + 1) * 128, :], flat(solved_all)) * keep
            value = value.astype(BF16).reshape(8, 16, 128)
            if k == 0:
                u0_out[t * 8:(t + 1) * 8] = value
            else:
                u12_out[t * 8:(t + 1) * 8, (k - 1) * 16:k * 16] = value

    update(0)
    u0_in[l] = u0_out[l]
    to_leaf(X_U0, LEAF, 0, l, lambda q: u0_out.at[q], u0_in.at[l])
    update(1)
    update(2)
    u12_in[l] = u12_out[l]
    arrived(X_WEIGHT, weight.at[pl.ds(0, LEAF - 1)])
    arrived(X_U0, u0_in.at[pl.ds(0, LEAF - 1)])

    def collect(d, sums):
        w = weight[d].astype(F32)
        u = u0_in[d].astype(F32)
        return tuple(s - w[g:g + 1, :] * u for g, s in enumerate(sums))

    sums = lax.fori_loop(0, LEAF, collect, tuple(tops[g].astype(F32) for g in range(4)))
    for g in range(4):
        gright_out[g] = sums[g].astype(BF16)
    gright[l] = gright_out[l // 8]
    to_leaf(X_GRIGHT, LEAF, 0, l, lambda q: gright_out.at[q // 8], gright.at[l])
    to_leaf(X_U12, LEAF, 0, l, lambda q: u12_out.at[q], u12_in.at[l])
    arrived(X_GRIGHT, gright.at[pl.ds(0, LEAF - 1)])
    scattered(dot(grand[...], flat(gright)), gred_out)
    gred[p] = gred_out[p]
    to_panel(X_GRED, lambda q: gred_out.at[q], gred.at[p])
    arrived(X_U12, u12_in.at[pl.ds(0, LEAF - 1)])

    def collect12(d, sums):
        w = weight[d].astype(F32)
        u = u12_in[d].astype(F32)
        return (sums[0] - w[4:5, :] * u[0:16], sums[1] - w[5:6, :] * u[0:16], sums[2] - u[16:32])

    sums = lax.fori_loop(0, LEAF, collect12, tuple(tops[g].astype(F32) for g in range(4, 7)))
    ctop_out[0] = sums[0].astype(BF16)
    ctop_out[1] = sums[1].astype(BF16)
    root_top = sums[2]
    for c in range(2):
        owner = 16 * c + l // 2
        half = l - l // 2 * 2

        @pl.when(owner == l)
        def _():
            ctop[half] = ctop_out[c]

        @pl.when(owner != l)
        def _():
            send(X_CTOP, ctop_out.at[c], ctop.at[half], (owner, p))

    arrived(X_GRED, gred.at[pl.ds(0, PANEL - 1)])
    gsol[p] = total(gred).astype(BF16)
    to_panel(X_GSOL, lambda q: gsol.at[p], gsol.at[p])
    loads[3].wait()
    loads[4].wait()
    loads[6].wait()
    arrived(X_GSOL, gsol.at[pl.ds(0, PANEL - 1)])

    scattered(dot(cp[...], flat(gsol)), cred_out)
    cred[m16] = cred_out[m16]
    to_leaf(X_CRED, 16, l16, m16, lambda q: cred_out.at[q], cred.at[m16])
    rg_part[...] = dot(rg[...], flat(gsol))
    source_self = jnp.logical_or(l == 0, l == LEAF - 1)

    @pl.when(source_self)
    def _():
        arrived(X_CTOP, ctop.at[0])

    @pl.when(jnp.logical_not(source_self))
    def _():
        arrived(X_CTOP, ctop)

    arrived(X_CRED, cred.at[pl.ds(0, 15)])
    cright[m16] = (flat(ctop).astype(F32) - total(cred)).astype(BF16)
    to_leaf(X_CRIGHT, 16, l16, m16, lambda q: cright.at[m16], cright.at[m16])
    arrived(X_CRIGHT, cright.at[pl.ds(0, 15)])
    scattered(dot(child[...], flat(cright)), cred2_out)
    cred2[p] = cred2_out[p]
    to_panel(X_CRED2, lambda q: cred2_out.at[q], cred2.at[p])
    arrived(X_CRED2, cred2.at[pl.ds(0, PANEL - 1)])
    csol[p] = total(cred2).astype(BF16)
    to_panel(X_CSOL, lambda q: csol.at[p], csol.at[p])
    arrived(X_CSOL, csol.at[pl.ds(0, PANEL - 1)])

    scattered(dot(rc[...], flat(csol)) + rg_part[...], rred_out)
    rred[l] = rred_out[l]
    to_leaf(X_RRED, LEAF, 0, l, lambda q: rred_out.at[q], rred.at[l])
    arrived(X_RRED, rred.at[pl.ds(0, LEAF - 1)])
    rright[l] = (root_top - total(rred)).astype(BF16)
    to_leaf(X_RRIGHT, LEAF, 0, l, lambda q: rright.at[l], rright.at[l])
    arrived(X_RRIGHT, rright.at[pl.ds(0, LEAF - 1)])
    scattered(dot(root[...], flat(rright)), rred2_out)
    rred2[p] = rred2_out[p]
    to_panel(X_RRED2, lambda q: rred2_out.at[q], rred2.at[p])
    arrived(X_RRED2, rred2.at[pl.ds(0, PANEL - 1)])
    rsol[p] = total(rred2).astype(BF16)
    to_panel(X_RSOL, lambda q: rsol.at[p], rsol.at[p])
    arrived(X_RSOL, rsol.at[pl.ds(0, PANEL - 1)])
    scattered(dot_t(root[...], flat(rsol)), rback_out)
    rback[l] = rback_out[l]
    to_leaf(X_RBACK, LEAF, 0, l, lambda q: rback_out.at[q], rback.at[l])
    arrived(X_RBACK, rback.at[pl.ds(0, LEAF - 1)])
    rres[l] = total(rback).astype(BF16)
    top_out[6] = rres[l]
    to_leaf(X_RRES, LEAF, 0, l, lambda q: rres.at[l], rres.at[l])
    arrived(X_RRES, rres.at[pl.ds(0, LEAF - 1)])

    scattered(dot_t(rc[...], flat(rres)), cback_out)
    cback[p] = cback_out[p]
    to_panel(X_CBACK, lambda q: cback_out.at[q], cback.at[p])
    gb_part[...] = dot_t(rg[...], flat(rres))
    arrived(X_CBACK, cback.at[pl.ds(0, PANEL - 1)])
    cresid[p] = (csol[p].astype(F32) - total(cback)).astype(BF16)
    to_panel(X_CRESID, lambda q: cresid.at[p], cresid.at[p])

    def masked(k, value):
        for t in range(4):
            keep = tiles[0, k, p * 4 + t].astype(F32)
            ancestor[t * 128:(t + 1) * 128] = (value[t * 128:(t + 1) * 128] * keep).astype(BF16)

    def pull_from(k, first):
        for n in range(8):
            at = slice(n * 256, (n + 1) * 256)
            value = dot_t(panels[k, :, at], ancestor[...])
            pulled[at, :] = value if first else pulled[at, :] + value

    arrived(X_CRESID, cresid.at[pl.ds(0, PANEL - 1)])
    scattered(dot_t(child[...], flat(cresid)), cback2_out)
    cback2[m16] = cback2_out[m16]
    to_leaf(X_CBACK2, 16, l16, m16, lambda q: cback2_out.at[q], cback2.at[m16])
    masked(2, flat(rres).astype(F32))
    pull_from(2, True)
    arrived(X_CBACK2, cback2.at[pl.ds(0, 15)])
    cres[m16] = total(cback2).astype(BF16)
    to_leaf(X_CRES, 16, l16, m16, lambda q: cres.at[m16], cres.at[m16])

    def to_far(k, c):
        send(X_CFAR, cres.at[m16], cfar.at[m16], (16 - l16 + lax.rem(m16 + k, 16), p))
        return c

    lax.fori_loop(0, 16, to_far, 0)
    arrived(X_CRES, cres.at[pl.ds(0, 15)])

    scattered(dot_t(cp[...], flat(cres)) + gb_part[...], gback_out)
    gback[p] = gback_out[p]
    to_panel(X_GBACK, lambda q: gback_out.at[q], gback.at[p])
    arrived(X_GBACK, gback.at[pl.ds(0, PANEL - 1)])
    gresid[p] = (gsol[p].astype(F32) - total(gback)).astype(BF16)
    to_panel(X_GRESID, lambda q: gresid.at[p], gresid.at[p])
    arrived(X_GRESID, gresid.at[pl.ds(0, PANEL - 1)])
    scattered(dot_t(grand[...], flat(gresid)), gback2_out)
    gback2[m8] = gback2_out[m8]
    to_leaf(X_GBACK2, 8, l8, m8, lambda q: gback2_out.at[q], gback2.at[m8])
    arrived(X_CFAR, cfar)
    near = jnp.where(l < 16, 1.0, 0.0).astype(F32)
    from_near = own_child[0] * near + own_child[1] * (1.0 - near)
    masked(1, flat(cres).astype(F32) * from_near + flat(cfar).astype(F32) * (1.0 - from_near))
    pull_from(1, False)
    near16 = near.astype(F32)
    at16 = pl.ds(pl.multiple_of(lax.rem(l, 2) * 16, 16), 16)
    here = cres[l // 2, at16].astype(F32)
    there = cfar[l // 2, at16].astype(F32)
    top_out[4] = (here * near16 + there * (1.0 - near16)).astype(BF16)
    top_out[5] = (there * near16 + here * (1.0 - near16)).astype(BF16)
    arrived(X_GBACK2, gback2.at[pl.ds(0, 7)])
    gres[l] = total(gback2).astype(BF16)
    to_leaf(X_GRES, LEAF, 0, l, lambda q: gres.at[l], gres.at[l])
    arrived(X_GRES, gres.at[pl.ds(0, LEAF - 1)])

    def grand_of(g):
        return gres[g * 8:(g + 1) * 8].reshape(512, 128).astype(F32)

    masked(0, sum(grand_of(g) * own_grand[g] for g in range(4)))
    at64 = pl.ds(pl.multiple_of(lax.rem(l, 4) * 16, 16), 16)
    for g in range(4):
        top_out[g] = gres[g * 8 + l // 4, at64]
    for n in range(8):
        at = slice(n * 256, (n + 1) * 256)
        pull_out[n] = (pulled[at, :] + dot_t(panels[0, :, at], ancestor[...])).astype(BF16)
    pull[p] = pull_out[p]
    to_panel(X_PULL, lambda q: pull_out.at[q], pull.at[p])
    arrived(X_PULL, pull.at[pl.ds(0, PANEL - 1)])
    residual = (solved_all[p].astype(F32) - total(pull)).astype(BF16)
    for n in range(8):
        leafo_out[n] = dot_t(inverse[:, n * 256:(n + 1) * 256], residual).astype(BF16)
    leafo[p] = leafo_out[p]
    to_panel(X_OUT, lambda q: leafo_out.at[q], leafo.at[p])
    arrived(X_OUT, leafo.at[pl.ds(0, PANEL - 1)])
    leaf_out[...] = total(leafo).astype(BF16)

    def sent(x, ref):
        pltpu.make_async_copy(ref, ref, send_sem.at[x]).wait()

    for x, ref, n in [
        (X_SIDES, sides_all, 7), (X_WEIGHT, weight, 31), (X_SOLVED, solved_all, 7), (X_U0, u0_in, 31), (X_U12, u12_in, 31),
        (X_GRIGHT, gright, 31), (X_GRED, gred, 7), (X_GSOL, gsol, 7), (X_CRED, cred, 15), (X_CRIGHT, cright, 15),
        (X_CRED2, cred2, 7), (X_CSOL, csol, 7), (X_RRED, rred, 31), (X_RRIGHT, rright, 31), (X_RRED2, rred2, 7),
        (X_RSOL, rsol, 7), (X_RBACK, rback, 31), (X_RRES, rres, 31), (X_CBACK, cback, 7), (X_CRESID, cresid, 7),
        (X_CBACK2, cback2, 15), (X_CRES, cres, 15), (X_CFAR, cfar, 16), (X_GBACK, gback, 7), (X_GRESID, gresid, 7),
        (X_GBACK2, gback2, 7), (X_GRES, gres, 31), (X_PULL, pull, 7), (X_OUT, leafo, 7),
    ]:
        sent(x, ref.at[pl.ds(0, n)])

    @pl.when(source_self)
    def _():
        sent(X_CTOP, ctop.at[0])

    @pl.when(jnp.logical_not(source_self))
    def _():
        sent(X_CTOP, ctop)


def per_device(
    leaf_sides, leaf_inverse, leaf_panels, parent_map, tile_mask, top_sides,
    grand_inverse, child_inverse, root_inverse, child_panels, root_grand, root_child,
):
    def bf(*shape):
        return pltpu.VMEM(shape, BF16)

    def pieces(n, rows):
        return bf(n, rows, 128)

    vmem = pl.BlockSpec(memory_space=pltpu.VMEM)
    smem = pl.BlockSpec(memory_space=pltpu.SMEM)
    hbm = pl.BlockSpec(memory_space=pl.ANY)
    scratch = [
        bf(256, 2048), bf(3, 512, 2048), bf(512, 512), bf(256, 512), bf(128, 512), bf(512, 512), bf(512, 512), bf(512, 256),
        pltpu.SemaphoreType.DMA((8,)), pltpu.SemaphoreType.DMA((X_COUNT,)), pltpu.SemaphoreType.DMA((X_COUNT,)),
        pieces(8, 256), pieces(32, 16), pieces(8, 256), pieces(32, 16), pieces(32, 32), pieces(32, 16), pieces(32, 32),
        pieces(4, 16), pieces(32, 16), pieces(8, 64), pieces(8, 64), pieces(8, 64),
        pieces(2, 16), pieces(2, 16), pieces(16, 32), pieces(16, 32), pieces(16, 32),
        pieces(8, 32), pieces(8, 32), pieces(8, 32),
        pieces(32, 16), pieces(32, 16), pieces(32, 16),
        pieces(8, 16), pieces(8, 16), pieces(8, 16),
        pieces(32, 16), pieces(32, 16), pieces(32, 16),
        pieces(8, 32), pieces(8, 32), pieces(8, 32),
        pieces(16, 32), pieces(16, 32), pieces(16, 32), pieces(16, 32),
        pieces(8, 64), pieces(8, 64), pieces(8, 64),
        pieces(8, 64), pieces(8, 64), pieces(32, 64),
        pltpu.VMEM((2048, 128), F32), pieces(8, 256), pieces(8, 256), pieces(8, 256), pieces(8, 256),
        bf(512, 128), pltpu.VMEM((512, 128), F32), pltpu.VMEM((512, 128), F32),
    ]
    return pl.pallas_call(
        kernel,
        out_shape=(jax.ShapeDtypeStruct((256, 128), BF16), jax.ShapeDtypeStruct((7, 16, 128), BF16)),
        in_specs=[smem, smem, vmem, hbm, hbm, vmem, hbm, hbm, hbm, hbm, hbm, hbm],
        out_specs=(vmem, vmem),
        scratch_shapes=scratch,
        compiler_params=pltpu.CompilerParams(collective_id=0, has_side_effects=True, vmem_limit_bytes=40 << 20),
        cost_estimate=pl.CostEstimate(flops=2_400_000_000, bytes_accessed=12_000_000, transcendentals=0),
        name="solve",
    )(
        parent_map, tile_mask, leaf_sides, leaf_inverse, leaf_panels, top_sides,
        grand_inverse, child_inverse, root_inverse, child_panels, root_grand, root_child,
    )


def solution(mesh):
    placed = (
        P(("leaf", "panel"), None),
        P(("leaf", "panel"), None),
        P(None, "panel", "leaf"),
        P("leaf"),
        P("leaf", None, None),
        P(None, ("panel", "leaf"), None),
        P("leaf", "panel"),
        P("leaf", "panel"),
        P("leaf", "panel"),
        P("panel", "leaf"),
        P("panel", "leaf"),
        P("panel", "leaf"),
    )
    return jax.shard_map(
        per_device,
        mesh=mesh,
        in_specs=placed,
        out_specs=(P(("leaf", "panel"), None), P(None, ("panel", "leaf"), None)),
        check_vma=False,
    )
```

```python
import functools

import jax
import jax.numpy as jnp
from jax import lax
from jax.experimental import pallas as pl
from jax.experimental.pallas import tpu as pltpu
from jax.sharding import PartitionSpec as P

MESH = pl.DeviceIdType.MESH
F32 = jnp.float32
BF16 = jnp.bfloat16
LEAF = 32
PANEL = 8
VMEM_BYTES = 60 << 20

NAMES = (
    "SIDES", "SIDES_PAIR", "WEIGHT", "SOLVED", "SOLVED_PAIR", "U0", "GRIGHT", "GRED", "GSOL", "CHILD", "RC", "RLINE", "CTOP",
    "CRED", "CRIGHT", "CSIB", "RTOP", "RRED", "RRIGHT", "RSIB", "RBACK", "RRES", "RNAT", "CRSIB", "CBACK", "CRES", "CFAR",
    "GBACK", "GRESID", "GBACK2", "GRES", "PULL", "OUT",
)
X = {name: i for i, name in enumerate(NAMES)}


def lower_mask(ref, out, row0, col0, tile):
    rows, cols = ref.shape

    def body(i, c):
        at = pl.ds(pl.multiple_of(i * tile, tile), tile)
        row = row0 + i * tile + lax.broadcasted_iota(jnp.int32, (tile, cols), 0)
        col = col0 + lax.broadcasted_iota(jnp.int32, (tile, cols), 1)
        out[at, :] = jnp.where(row >= col, ref[at, :].astype(F32), 0.0).astype(BF16)
        return c

    lax.fori_loop(0, rows // tile, body, 0)


def dot(a, b):
    return jnp.dot(a, b, preferred_element_type=F32)


def dot_t(a, b):
    return lax.dot_general(a, b, (((0,), (0,)), ((), ())), preferred_element_type=F32)


def dot_nt(a, b):
    return lax.dot_general(a, b, (((1,), (1,)), ((), ())), preferred_element_type=F32)


def kernel(
    parent, tiles, sides_h, inverse_h, panels_h, tops_h, grand_h, child_h, root_h, cp_h, rg_h, rc_h,
    leaf_out, top_out,
    inverse, panels, grand, child_all, root, cp, rg, rc_all,
    in_sem, send_sem, recv_sem, pair_sem, z_sem, z_send_sem, round_sem,
    sides_all, tops, weight, solved_all, u0_out, u0_in, u1_part, u2_part, work,
    gright_out, gright, gred_out, gred, gsol, ctop_out, ctop, cred_out, cred, cpiece, cright, cs_out, cs_in, cs,
    rtop_out, rtop, rred_out, rred, rright, rs_out, rs_in, rs, rback_out, rback, rres, rnat, cr_out, cr_in,
    cback_out, cback, cres_piece, cnat, cfar, gback_out, gback, gresid, gback2_out, gback2, gres,
    pulled, pull_out, pull, leafo_out, leafo, ancestor, gb_part, inverse_t, panel_t, root_nat, child_nat, far_nat,
):
    l = lax.axis_index("leaf")
    p = lax.axis_index("panel")
    l8, l16 = l // 8 * 8, l // 16 * 16
    m8, m16 = l - l8, l - l16
    y = p // 2
    core = p - 2 * y
    own_y = m16 // 4
    own_i = m16 - 4 * own_y
    diag = own_y == y
    root_y = l // 8
    root_i = (l - 8 * root_y) // 2
    root_half = l - l // 2 * 2
    root_diag = root_y == y

    loads = []
    for i, (src, dst) in enumerate(
        [(inverse_h, inverse), (panels_h, panels), (grand_h, grand), (child_h, child_all.at[y]), (root_h, root.at[y]), (cp_h, cp), (rg_h, rg), (rc_h, rc_all.at[y]), (tops_h, tops), (sides_h, sides_all.at[p])]
    ):
        loads.append(pltpu.make_async_copy(src, dst, in_sem.at[i]))
    loads[9].start()
    loads[0].start()
    loads[8].start()

    barrier = pltpu.get_barrier_semaphore()

    x_of = lax.rem(l, 4)
    x_peers = [l - x_of + lax.rem(x_of + k, 4) for k in range(1, 4)]
    z_peers = {k: lax.rem(l + 4 * k, LEAF) for k in range(1, 8)}

    def signal(semaphore, leaf, panel):
        pl.semaphore_signal(semaphore, inc=1, device_id=(leaf, panel), device_id_type=MESH)

    for k in range(1, PANEL):
        signal(barrier, l, lax.rem(p + k, PANEL))
    for there in x_peers + [z_peers[1], z_peers[7]]:
        signal(barrier, there, p)

    def send(x, src, dst, device):
        pltpu.make_async_remote_copy(src, dst, send_sem.at[X[x]], recv_sem.at[X[x]], device_id=device, device_id_type=MESH).start()

    def arrived(x, ref):
        pltpu.make_async_copy(ref, ref, recv_sem.at[X[x]]).wait()

    def to_panel(x, src_of, dst):
        def body(k, c):
            q = lax.rem(p + k, PANEL)
            send(x, src_of(q), dst, (l, q))
            return c

        lax.fori_loop(1, PANEL, body, 0)

    def to_leaf(x, n, base, me, src_of, dst):
        def body(k, c):
            q = lax.rem(me + k, n)
            send(x, src_of(q), dst, (base + q, p))
            return c

        lax.fori_loop(n // 2, n, body, 0)
        lax.fori_loop(1, n // 2, body, 0)

    def total(ref):
        return jnp.sum(ref[...].astype(F32), axis=0)

    def flat(ref):
        return ref[...].reshape(ref.shape[0] * ref.shape[1], ref.shape[2])

    def scattered(value, out):
        out[...] = value.astype(BF16).reshape(out.shape)

    def arrived_but_self(x, ref, has_self, n):
        @pl.when(has_self)
        def _():
            arrived(x, ref.at[pl.ds(0, n - 1)])

        @pl.when(jnp.logical_not(has_self))
        def _():
            arrived(x, ref.at[pl.ds(0, n)])

    def to_line(x, n, base, me, src, dst, q):
        def body(k, c):
            there = base + lax.rem(me + k, n)

            @pl.when(jnp.logical_or(there != l, q != p))
            def _():
                send(x, src, dst, (there, q))

            return c

        lax.fori_loop(n // 2, n, body, 0)
        lax.fori_loop(0, n // 2, body, 0)

    def to_sibling(x, src, dst):
        send(x, src, dst, (l, p + 1 - 2 * core))

    def to_chips(x, src, dst):
        def body(k, c):
            send(x, src, dst, (l, lax.rem(p + 2 * k, PANEL)))
            return c

        lax.fori_loop(1, 4, body, 0)

    def gather_panel(which, x, ref, beside):
        to_chips_each(which, x, ref)
        to_sibling(x + "_PAIR", ref.at[p], ref.at[p])
        beside()
        for k in range(1, 4):
            came = lax.rem(p + PANEL - 2 * k, PANEL)
            pltpu.make_async_copy(ref.at[came], ref.at[came], pair_sem.at[which, k]).wait()
            to_sibling(x + "_PAIR", ref.at[came], ref.at[came])
        arrived(x + "_PAIR", ref.at[pl.ds(0, 4)])

    def to_chips_each(which, x, ref):
        for k in range(1, 4):
            pltpu.make_async_remote_copy(
                ref.at[p], ref.at[p], send_sem.at[X[x]], pair_sem.at[which, k],
                device_id=(l, lax.rem(p + 2 * k, PANEL)), device_id_type=MESH,
            ).start()

    def cut(value, store):
        value = value.astype(BF16)
        for j in range(4):
            for i in range(4):
                store(4 * j + i, value[32 * j:32 * j + 32, 128 * i:128 * i + 128])

    def strip(ref, j):
        return jnp.concatenate([ref[4 * j + i] for i in range(4)], axis=1)

    def put_strip(ref, j, value):
        value = value.astype(BF16)
        for i in range(4):
            ref[4 * j + i] = value[:, 128 * i:128 * i + 128]

    def strip2(ref, j):
        return jnp.concatenate(
            [jnp.concatenate([ref[8 * j + 2 * i], ref[8 * j + 2 * i + 1]], axis=0) for i in range(4)], axis=1
        )

    def put_strip2(ref, j, value):
        value = value.astype(BF16)
        for i in range(4):
            for h in range(2):
                ref[8 * j + 2 * i + h] = value[16 * h:16 * h + 16, 128 * i:128 * i + 128]

    def natural(src, dst):
        n = src.shape[0] // 4
        for i in range(4):
            block = jnp.concatenate([src[n * i + j] for j in range(n)], axis=0).astype(F32)
            dst[128 * i:128 * i + 128] = block.T.astype(BF16)

    mine = parent[0]
    own_grand = [jnp.where(mine == g, 1.0, 0.0).astype(F32) for g in range(4)]
    own_child = [own_grand[0] + own_grand[1], own_grand[2] + own_grand[3]]
    slot = lax.broadcasted_iota(jnp.int32, (16, 128), 0)
    picks = jnp.zeros((16, 128), F32)
    for g in range(4):
        picks = picks + jnp.where(slot == g, own_grand[g], 0.0)
    weight[l] = picks.astype(BF16)
    share = pl.ds(pl.multiple_of(l * 16, 16), 16)

    pl.semaphore_wait(barrier, PANEL - 1 + 5)
    loads[9].wait()

    def first_rounds():
        for there in (z_peers[1], z_peers[7]):
            signal(round_sem.at[0], there, p)
        loads[1].start()
        loads[0].wait()
        lower_mask(inverse, inverse, p * 256, 0, 32)
        pl.semaphore_wait(round_sem.at[0], 2)
        for there in (z_peers[2], z_peers[6]):
            signal(round_sem.at[1], there, p)

    gather_panel(0, "SIDES", sides_all, first_rounds)
    solved_all[p] = dot(inverse[...], flat(sides_all)).astype(BF16)

    def last_round():
        pl.semaphore_wait(round_sem.at[1], 2)
        for there in x_peers:
            signal(round_sem.at[2], there, p)
        for copy in loads[2:8]:
            copy.start()
        loads[1].wait()
        loads[2].wait()
        lower_mask(grand, grand, m8 * 512, p * 512, 64)

    gather_panel(1, "SOLVED", solved_all, last_round)
    pl.semaphore_wait(round_sem.at[2], 3)

    loads[8].wait()

    def update(k, t):
        keep = tiles[0, k, p * 4 + t].astype(F32)
        return dot(panels[k, t * 128:(t + 1) * 128, :], flat(solved_all)) * keep

    for t in range(4):
        u0_out[t * 8:(t + 1) * 8] = update(0, t).astype(BF16).reshape(8, 16, 128)
    u0_in[l] = u0_out[l]
    to_leaf("U0", LEAF, 0, l, lambda q: u0_out.at[q], u0_in.at[l])
    to_leaf("WEIGHT", LEAF, 0, l, lambda q: weight.at[l], weight.at[l])
    loads[3].wait()
    lower_mask(child_all.at[y], child_all.at[y], m16 * 256, p * 512, 64)
    loads[4].wait()
    lower_mask(root.at[y], root.at[y], l * 128, p * 512, 64)
    to_chips("CHILD", child_all.at[y], child_all.at[y])

    to_chips("RLINE", root.at[y], root.at[y])
    for t in range(4):
        at = slice(t * 128, (t + 1) * 128)
        u1_part[at] = update(1, t)
        u2_part[at] = update(2, t)
    u2_part[share] = u2_part[share] - tops[6].astype(F32)
    for c in range(2):
        work[...] = u1_part[...] * own_child[c]
        work[share] = work[share] - tops[4 + c].astype(F32)

        def store(j, v):
            ctop_out[16 * c + j] = v

        cut(work[...].T, store)
    ctop[l] = ctop_out[l]
    arrived("WEIGHT", weight.at[pl.ds(0, LEAF - 1)])
    arrived("U0", u0_in.at[pl.ds(0, LEAF - 1)])

    def collect(d, sums):
        w = weight[d].astype(F32)
        u = u0_in[d].astype(F32)
        return tuple(s - w[g:g + 1, :] * u for g, s in enumerate(sums))

    sums = lax.fori_loop(0, LEAF, collect, tuple(tops[g].astype(F32) for g in range(4)), unroll=4)
    for g in range(4):
        gright_out[g] = sums[g].astype(BF16)
    gright[l] = gright_out[l // 8]
    to_leaf("GRIGHT", LEAF, 0, l, lambda q: gright_out.at[q // 8], gright.at[l])
    to_leaf("CTOP", LEAF, 0, l, lambda q: ctop_out.at[q], ctop.at[l])
    arrived("GRIGHT", gright.at[pl.ds(0, LEAF - 1)])
    scattered(dot(grand[...], flat(gright)), gred_out)
    gred[p] = gred_out[p]
    to_panel("GRED", lambda q: gred_out.at[q], gred.at[p])
    arrived("CTOP", ctop.at[pl.ds(0, LEAF - 1)])
    cpiece[...] = total(ctop)
    arrived("GRED", gred.at[pl.ds(0, PANEL - 1)])
    gsol[p] = total(gred).astype(BF16)
    to_panel("GSOL", lambda q: gsol.at[p], gsol.at[p])
    for i in range(5, 8):
        loads[i].wait()
    arrived("GSOL", gsol.at[pl.ds(0, PANEL - 1)])

    def store(j, v):
        cred_out[j] = v

    cut(dot(cp[...], flat(gsol)).T, store)
    cred[m16] = cred_out[m16]
    to_leaf("CRED", 16, l16, m16, lambda q: cred_out.at[q], cred.at[m16])
    to_chips("RC", rc_all.at[y], rc_all.at[y])

    back = (dot(rg[...], flat(gsol)) + u2_part[...]).T.astype(BF16)
    for j in range(4):
        for i in range(4):
            for h in range(2):
                at = 32 * j + 16 * h
                rtop_out[8 * j + 2 * i + h] = back[at:at + 16, 128 * i:128 * i + 128]

    arrived("CRED", cred.at[pl.ds(0, 15)])
    cres_piece[0] = (-(cpiece[...] + total(cred))).astype(BF16)
    to_line("CRIGHT", 16, l16, m16, cres_piece.at[0], cright.at[4 * y + own_i], 2 * own_y + core)

    @pl.when(diag)
    def _():
        cright[4 * y + own_i] = cres_piece[0]

    def to_rtop(k, c):
        j = lax.rem(k, 4)
        there = 8 * y + k // 4
        q = 2 * j + core

        @pl.when(jnp.logical_or(there != l, q != p))
        def _():
            send("RTOP", rtop_out.at[8 * j + k // 4], rtop.at[l], (there, q))

        return c

    lax.fori_loop(0, 32, to_rtop, 0)

    @pl.when(root_diag)
    def _():
        rtop[l] = rtop_out[l]

    arrived("CHILD", child_all.at[pl.ds(0, 3)])
    arrived_but_self("CRIGHT", cright, diag, 16)

    def summed(x, value, out, inbox):
        out[...] = value.astype(BF16)
        to_sibling(x, out, inbox)
        arrived(x, inbox)
        return out[...].astype(F32) + inbox[...].astype(F32)

    cs[...] = summed("CSIB", sum(dot_nt(strip(cright, j), child_all[j]) for j in range(4)), cs_out, cs_in).astype(BF16)
    arrived("RC", rc_all.at[pl.ds(0, 3)])

    for j in range(4):
        put_strip2(rred_out, j, dot_nt(cs[...], rc_all[j]))
    rred[l] = rred_out[l]
    to_leaf("RRED", LEAF, 0, l, lambda q: rred_out.at[q], rred.at[l])
    for n in range(8):
        at = slice(n * 256, (n + 1) * 256)
        inverse_t[at, :] = inverse[:, at].T
    arrived_but_self("RTOP", rtop, root_diag, 32)
    root_top = total(rtop)
    arrived("RLINE", root.at[pl.ds(0, 3)])
    arrived("RRED", rred.at[pl.ds(0, LEAF - 1)])
    rright[l] = (-(root_top + total(rred))).astype(BF16)
    to_leaf("RRIGHT", LEAF, 0, l, lambda q: rright.at[l], rright.at[l])
    for n in range(8):
        at = slice(n * 256, (n + 1) * 256)
        panel_t[at, :] = panels[0, :, at].T
    arrived("RRIGHT", rright.at[pl.ds(0, LEAF - 1)])
    rs[...] = summed("RSIB", sum(dot_nt(strip2(rright, j), root[j]) for j in range(4)), rs_out, rs_in).astype(BF16)
    for j in range(4):
        put_strip2(rback_out, j, dot(rs[...], root[j]))
    rback[l] = rback_out[l]
    to_leaf("RBACK", LEAF, 0, l, lambda q: rback_out.at[q], rback.at[l])
    arrived("RBACK", rback.at[pl.ds(0, LEAF - 1)])
    rres[l] = total(rback).astype(BF16)
    to_leaf("RRES", LEAF, 0, l, lambda q: rres.at[l], rres.at[l])
    rnat_at = 8 * root_i + 2 * y + root_half
    to_line("RNAT", LEAF, 0, l, rres.at[l], rnat.at[rnat_at], 2 * root_y + core)

    @pl.when(root_diag)
    def _():
        rnat[rnat_at] = rres[l]

    arrived("RRES", rres.at[pl.ds(0, LEAF - 1)])

    crs = summed("CRSIB", sum(dot(strip2(rres, j), rc_all[j]) for j in range(4)), cr_out, cr_in)
    residual_c = (cs[...].astype(F32) - crs).astype(BF16)
    for j in range(4):
        put_strip(cback_out, j, dot(residual_c, child_all[j]))
    cback[m16] = cback_out[m16]
    to_leaf("CBACK", 16, l16, m16, lambda q: cback_out.at[q], cback.at[m16])

    def masked(k, value):
        for t in range(4):
            keep = tiles[0, k, p * 4 + t].astype(F32)
            ancestor[t * 128:(t + 1) * 128] = (value[t * 128:(t + 1) * 128] * keep).astype(BF16)

    def pull_from(k, first):
        for n in range(8):
            at = slice(n * 256, (n + 1) * 256)
            value = dot_t(panels[k, :, at], ancestor[...])
            pulled[at, :] = value if first else pulled[at, :] + value

    arrived_but_self("RNAT", rnat, root_diag, 32)
    natural(rnat, root_nat)
    gb_part[...] = dot_t(rg[...], root_nat[...])
    arrived("CBACK", cback.at[pl.ds(0, 15)])
    cres_piece[1] = total(cback).astype(BF16)
    to_line("CRES", 16, l16, m16, cres_piece.at[1], cnat.at[4 * own_i + y], 2 * own_y + core)
    to_line("CFAR", 16, 16 - l16, m16, cres_piece.at[1], cfar.at[4 * own_i + y], 2 * own_y + core)

    @pl.when(diag)
    def _():
        cnat[4 * own_i + y] = cres_piece[1]

    top_out[6] = root_nat[share]
    masked(2, root_nat[...].astype(F32))
    pull_from(2, True)
    arrived_but_self("CRES", cnat, diag, 16)
    natural(cnat, child_nat)

    scattered(dot_t(cp[...], child_nat[...]) + gb_part[...], gback_out)
    gback[p] = gback_out[p]
    to_panel("GBACK", lambda q: gback_out.at[q], gback.at[p])
    arrived("CFAR", cfar)
    natural(cfar, far_nat)
    arrived("GBACK", gback.at[pl.ds(0, PANEL - 1)])
    gresid[p] = (gsol[p].astype(F32) - total(gback)).astype(BF16)
    to_panel("GRESID", lambda q: gresid.at[p], gresid.at[p])
    near = jnp.where(l < 16, 1.0, 0.0).astype(F32)
    here = child_nat[share].astype(F32)
    there = far_nat[share].astype(F32)
    top_out[4] = (here * near + there * (1.0 - near)).astype(BF16)
    top_out[5] = (there * near + here * (1.0 - near)).astype(BF16)
    from_near = own_child[0] * near + own_child[1] * (1.0 - near)
    masked(1, child_nat[...].astype(F32) * from_near + far_nat[...].astype(F32) * (1.0 - from_near))
    arrived("GRESID", gresid.at[pl.ds(0, PANEL - 1)])
    scattered(dot_t(grand[...], flat(gresid)), gback2_out)
    gback2[m8] = gback2_out[m8]
    to_leaf("GBACK2", 8, l8, m8, lambda q: gback2_out.at[q], gback2.at[m8])
    pull_from(1, False)
    arrived("GBACK2", gback2.at[pl.ds(0, 7)])
    gres[l] = total(gback2).astype(BF16)
    order = (4, 3, 5, 2, 6, 1, 7)
    for k in order:
        pltpu.make_async_remote_copy(
            gres.at[l], gres.at[l], z_send_sem, z_sem.at[k], device_id=(z_peers[k], p), device_id_type=MESH
        ).start()
    for there in x_peers:
        send("GRES", gres.at[l], gres.at[l], (there, p))
    for k in order[::-1]:
        came = z_peers[8 - k]
        pltpu.make_async_copy(gres.at[came], gres.at[came], z_sem.at[k]).wait()
        for there in x_peers:
            send("GRES", gres.at[came], gres.at[came], (there, p))
    arrived("GRES", gres.at[pl.ds(0, 24)])

    def grand_of(g):
        return gres[g * 8:(g + 1) * 8].reshape(512, 128).astype(F32)

    masked(0, sum(grand_of(g) * own_grand[g] for g in range(4)))
    at64 = pl.ds(pl.multiple_of(lax.rem(l, 4) * 16, 16), 16)
    for n in range(8):
        at = slice(n * 256, (n + 1) * 256)
        pull_out[n] = (pulled[at, :] + dot(panel_t[at, :], ancestor[...])).astype(BF16)
    pull[p] = pull_out[p]
    to_panel("PULL", lambda q: pull_out.at[q], pull.at[p])
    for g in range(4):
        top_out[g] = gres[g * 8 + l // 4, at64]
    arrived("PULL", pull.at[pl.ds(0, PANEL - 1)])
    residual = (solved_all[p].astype(F32) - total(pull)).astype(BF16)
    for n in range(8):
        leafo_out[n] = dot(inverse_t[n * 256:(n + 1) * 256, :], residual).astype(BF16)
    leafo[p] = leafo_out[p]
    to_panel("OUT", lambda q: leafo_out.at[q], leafo.at[p])
    arrived("OUT", leafo.at[pl.ds(0, PANEL - 1)])
    leaf_out[...] = total(leafo).astype(BF16)

    def sent(x, ref):
        pltpu.make_async_copy(ref, ref, send_sem.at[X[x]]).wait()

    for x, ref, n in [
        ("SIDES", sides_all, 3), ("SIDES_PAIR", sides_all, 4), ("SOLVED_PAIR", solved_all, 4), ("WEIGHT", weight, 31), ("SOLVED", solved_all, 3), ("U0", u0_in, 31), ("GRIGHT", gright, 31),
        ("GRED", gred, 7), ("GSOL", gsol, 7), ("CHILD", child_all, 3), ("RC", rc_all, 3), ("RLINE", root, 3), ("CTOP", ctop, 31), ("CRED", cred, 15),
        ("RRED", rred, 31), ("RRIGHT", rright, 31), ("RBACK", rback, 31), ("RRES", rres, 31), ("CBACK", cback, 15),
        ("CFAR", cfar, 16), ("GBACK", gback, 7), ("GRESID", gresid, 7), ("GBACK2", gback2, 7), ("GRES", gres, 24),
        ("PULL", pull, 7), ("OUT", leafo, 7),
    ]:
        sent(x, ref.at[pl.ds(0, n)])
    pltpu.make_async_copy(gres.at[pl.ds(0, 7)], gres.at[pl.ds(0, 7)], z_send_sem).wait()
    for x, ref in [("CSIB", cs_in), ("RSIB", rs_in), ("CRSIB", cr_in)]:
        sent(x, ref)

    @pl.when(diag)
    def _():
        for x, ref, n in [("CRIGHT", cright, 15), ("CRES", cnat, 15)]:
            sent(x, ref.at[pl.ds(0, n)])

    @pl.when(jnp.logical_not(diag))
    def _():
        for x, ref in [("CRIGHT", cright), ("CRES", cnat)]:
            sent(x, ref)

    @pl.when(root_diag)
    def _():
        for x, ref in [("RTOP", rtop), ("RNAT", rnat)]:
            sent(x, ref.at[pl.ds(0, 31)])

    @pl.when(jnp.logical_not(root_diag))
    def _():
        for x, ref in [("RTOP", rtop), ("RNAT", rnat)]:
            sent(x, ref)


def per_device(
    leaf_sides, leaf_inverse, leaf_panels, parent_map, tile_mask, top_sides,
    grand_inverse, child_inverse, root_inverse, child_panels, root_grand, root_child,
):
    def bf(*shape):
        return pltpu.VMEM(shape, BF16)

    def pieces(n, rows):
        return bf(n, rows, 128)

    vmem = pl.BlockSpec(memory_space=pltpu.VMEM)
    smem = pl.BlockSpec(memory_space=pltpu.SMEM)
    hbm = pl.BlockSpec(memory_space=pltpu.HBM)
    def f32(*shape):
        return pltpu.VMEM(shape, F32)

    sems = pltpu.SemaphoreType.DMA((len(X),))
    scratch = [
        bf(256, 2048), bf(3, 512, 2048), bf(512, 512), bf(4, 256, 512), bf(4, 128, 512),
        bf(512, 512), bf(512, 512), bf(4, 512, 256), pltpu.SemaphoreType.DMA((10,)), sems, sems,
        pltpu.SemaphoreType.DMA((2, 4)), pltpu.SemaphoreType.DMA((8,)), pltpu.SemaphoreType.DMA, pltpu.SemaphoreType.REGULAR((3,)),
        pieces(8, 256), bf(7, 16, 128), pieces(32, 16), pieces(8, 256), pieces(32, 16), pieces(32, 16),
        f32(512, 128), f32(512, 128), f32(512, 128),
        pieces(4, 16), pieces(32, 16), pieces(8, 64), pieces(8, 64), pieces(8, 64),
        pieces(32, 32), pieces(32, 32), pieces(16, 32), pieces(16, 32),
        f32(32, 128), pieces(16, 32), bf(32, 256), bf(32, 256), bf(32, 256),
        pieces(32, 16), pieces(32, 16), pieces(32, 16), pieces(32, 16), pieces(32, 16),
        bf(32, 128), bf(32, 128), bf(32, 128), pieces(32, 16), pieces(32, 16), pieces(32, 16),
        pieces(32, 16), bf(32, 256), bf(32, 256),
        pieces(16, 32), pieces(16, 32), pieces(2, 32), pieces(16, 32), pieces(16, 32),
        pieces(8, 64), pieces(8, 64), pieces(8, 64),
        pieces(8, 64), pieces(8, 64), pieces(32, 64),
        f32(2048, 128), pieces(8, 256), pieces(8, 256), pieces(8, 256), pieces(8, 256),
        bf(512, 128), f32(512, 128), bf(2048, 256), bf(2048, 512), bf(512, 128), bf(512, 128), bf(512, 128),
    ]
    return pl.pallas_call(
        kernel,
        out_shape=(jax.ShapeDtypeStruct((256, 128), BF16), jax.ShapeDtypeStruct((7, 16, 128), BF16)),
        in_specs=[smem, smem, hbm, hbm, hbm, hbm, hbm, hbm, hbm, hbm, hbm, hbm],
        out_specs=(vmem, vmem),
        scratch_shapes=scratch,
        compiler_params=pltpu.CompilerParams(collective_id=0, has_side_effects=True, vmem_limit_bytes=VMEM_BYTES),
        cost_estimate=pl.CostEstimate(flops=2_400_000_000, bytes_accessed=12_000_000, transcendentals=0),
        name="solve",
    )(
        parent_map, tile_mask, leaf_sides, leaf_inverse, leaf_panels, top_sides,
        grand_inverse, child_inverse, root_inverse, child_panels, root_grand, root_child,
    )


def solution(mesh):
    placed = (
        P(("leaf", "panel"), None),
        P(("leaf", "panel"), None),
        P(None, "panel", "leaf"),
        P("leaf"),
        P("leaf", None, None),
        P(None, ("panel", "leaf"), None),
        P("leaf", "panel"),
        P("leaf", "panel"),
        P("leaf", "panel"),
        P("panel", "leaf"),
        P("panel", "leaf"),
        P("panel", "leaf"),
    )
    return jax.shard_map(
        per_device,
        mesh=mesh,
        in_specs=placed,
        out_specs=(P(("leaf", "panel"), None), P(None, ("panel", "leaf"), None)),
        check_vma=False,
    )
```

```python
import functools

import jax
import jax.numpy as jnp
from jax import lax
from jax.experimental import pallas as pl
from jax.experimental.pallas import tpu as pltpu
from jax.sharding import PartitionSpec as P

MESH = pl.DeviceIdType.MESH
F32 = jnp.float32
BF16 = jnp.bfloat16
LEAF = 32
PANEL = 8
VMEM_BYTES = 60 << 20

NAMES = (
    "SIDES", "SIDES_PAIR", "WEIGHT", "SOLVED", "SOLVED_PAIR", "U0", "GRIGHT", "GRED", "GSOL", "CHILD", "RC", "RLINE", "CTOP",
    "CRED", "CRIGHT", "CSIB", "RTOP", "RRED", "RRIGHT", "RSIB", "RBACK", "RRES", "RNAT", "CRSIB", "CBACK", "CRES", "CFAR",
    "GBACK", "GRESID", "GBACK2", "GRES", "PULL", "OUT",
)
X = {name: i for i, name in enumerate(NAMES)}


def lower_mask(ref, out, row0, col0, tile):
    rows, cols = ref.shape

    def body(i, c):
        at = pl.ds(pl.multiple_of(i * tile, tile), tile)
        row = row0 + i * tile + lax.broadcasted_iota(jnp.int32, (tile, cols), 0)
        col = col0 + lax.broadcasted_iota(jnp.int32, (tile, cols), 1)
        out[at, :] = jnp.where(row >= col, ref[at, :].astype(F32), 0.0).astype(BF16)
        return c

    lax.fori_loop(0, rows // tile, body, 0)


def dot(a, b):
    return jnp.dot(a, b, preferred_element_type=F32)


def dot_t(a, b):
    return lax.dot_general(a, b, (((0,), (0,)), ((), ())), preferred_element_type=F32)


def dot_nt(a, b):
    return lax.dot_general(a, b, (((1,), (1,)), ((), ())), preferred_element_type=F32)


def kernel(
    parent, tiles_h, sides_h, inverse_h, panels_h, tops_h, grand_h, child_h, root_h, cp_h, rg_h, rc_h,
    leaf_out, top_out,
    inverse, panels, grand, child_all, root, cp, rg, rc_all,
    in_sem, send_sem, recv_sem, pair_sem, z_sem, z_send_sem, round_sem,
    sides_all, tops, tiles, weight, solved_all, u0_out, u0_in, u1_part, u2_part, work,
    gright_out, gright, gred_out, gred, gsol, ctop_out, ctop, cred_out, cred, cpiece, cright, cs_out, cs_in, cs,
    rtop_out, rtop, rred_out, rred, rright, rs_out, rs_in, rs, rback_out, rback, rres, rnat, cr_out, cr_in,
    cback_out, cback, cres_piece, cnat, cfar, gback_out, gback, gresid, gback2_out, gback2, gres,
    pulled, pull_out, pull, leafo_out, leafo, ancestor, gb_part, inverse_t, panel_t, root_nat, child_nat, far_nat,
):
    l = lax.axis_index("leaf")
    p = lax.axis_index("panel")
    l8, l16 = l // 8 * 8, l // 16 * 16
    m8, m16 = l - l8, l - l16
    y = p // 2
    core = p - 2 * y
    own_y = m16 // 4
    own_i = m16 - 4 * own_y
    diag = own_y == y
    root_y = l // 8
    root_i = (l - 8 * root_y) // 2
    root_half = l - l // 2 * 2
    root_diag = root_y == y

    loads = []
    for i, (src, dst) in enumerate(
        [(inverse_h, inverse), (panels_h, panels), (grand_h, grand), (child_h, child_all.at[y]), (root_h, root.at[y]), (cp_h, cp), (rg_h, rg), (rc_h, rc_all.at[y]), (tops_h, tops), (sides_h, sides_all.at[p]), (tiles_h, tiles)]
    ):
        loads.append(pltpu.make_async_copy(src, dst, in_sem.at[i]))
    loads[9].start()
    loads[0].start()
    loads[8].start()
    loads[10].start()

    barrier = pltpu.get_barrier_semaphore()

    x_of = lax.rem(l, 4)
    x_peers = [l - x_of + lax.rem(x_of + k, 4) for k in range(1, 4)]
    z_peers = {k: lax.rem(l + 4 * k, LEAF) for k in range(1, 8)}

    def signal(semaphore, leaf, panel):
        pl.semaphore_signal(semaphore, inc=1, device_id=(leaf, panel), device_id_type=MESH)

    for k in range(1, PANEL):
        signal(barrier, l, lax.rem(p + k, PANEL))
    for there in x_peers + [z_peers[1], z_peers[7]]:
        signal(barrier, there, p)

    def send(x, src, dst, device):
        pltpu.make_async_remote_copy(src, dst, send_sem.at[X[x]], recv_sem.at[X[x]], device_id=device, device_id_type=MESH).start()

    def arrived(x, ref):
        pltpu.make_async_copy(ref, ref, recv_sem.at[X[x]]).wait()

    def to_panel(x, src_of, dst):
        def body(k, c):
            q = lax.rem(p + k, PANEL)
            send(x, src_of(q), dst, (l, q))
            return c

        lax.fori_loop(1, PANEL, body, 0)

    def to_leaf(x, n, base, me, src_of, dst):
        def body(k, c):
            q = lax.rem(me + k, n)
            send(x, src_of(q), dst, (base + q, p))
            return c

        lax.fori_loop(n // 2, n, body, 0)
        lax.fori_loop(1, n // 2, body, 0)

    def total(ref):
        return jnp.sum(ref[...].astype(F32), axis=0)

    def flat(ref):
        return ref[...].reshape(ref.shape[0] * ref.shape[1], ref.shape[2])

    def scattered(value, out):
        out[...] = value.astype(BF16).reshape(out.shape)

    def arrived_but_self(x, ref, has_self, n):
        @pl.when(has_self)
        def _():
            arrived(x, ref.at[pl.ds(0, n - 1)])

        @pl.when(jnp.logical_not(has_self))
        def _():
            arrived(x, ref.at[pl.ds(0, n)])

    def to_line(x, n, base, me, src, dst, q):
        def body(k, c):
            there = base + lax.rem(me + k, n)

            @pl.when(jnp.logical_or(there != l, q != p))
            def _():
                send(x, src, dst, (there, q))

            return c

        lax.fori_loop(n // 2, n, body, 0)
        lax.fori_loop(0, n // 2, body, 0)

    def to_sibling(x, src, dst):
        send(x, src, dst, (l, p + 1 - 2 * core))

    def to_chips(x, src, dst):
        def body(k, c):
            send(x, src, dst, (l, lax.rem(p + 2 * k, PANEL)))
            return c

        lax.fori_loop(1, 4, body, 0)

    def gather_panel(which, x, ref, beside):
        to_chips_each(which, x, ref)
        to_sibling(x + "_PAIR", ref.at[p], ref.at[p])
        beside()
        for k in range(1, 4):
            came = lax.rem(p + PANEL - 2 * k, PANEL)
            pltpu.make_async_copy(ref.at[came], ref.at[came], pair_sem.at[which, k]).wait()
            to_sibling(x + "_PAIR", ref.at[came], ref.at[came])
        arrived(x + "_PAIR", ref.at[pl.ds(0, 4)])

    def to_chips_each(which, x, ref):
        for k in range(1, 4):
            pltpu.make_async_remote_copy(
                ref.at[p], ref.at[p], send_sem.at[X[x]], pair_sem.at[which, k],
                device_id=(l, lax.rem(p + 2 * k, PANEL)), device_id_type=MESH,
            ).start()

    def cut(value, store):
        value = value.astype(BF16)
        for j in range(4):
            for i in range(4):
                store(4 * j + i, value[32 * j:32 * j + 32, 128 * i:128 * i + 128])

    def strip(ref, j):
        return jnp.concatenate([ref[4 * j + i] for i in range(4)], axis=1)

    def put_strip(ref, j, value):
        value = value.astype(BF16)
        for i in range(4):
            ref[4 * j + i] = value[:, 128 * i:128 * i + 128]

    def strip2(ref, j):
        return jnp.concatenate(
            [jnp.concatenate([ref[8 * j + 2 * i], ref[8 * j + 2 * i + 1]], axis=0) for i in range(4)], axis=1
        )

    def put_strip2(ref, j, value):
        value = value.astype(BF16)
        for i in range(4):
            for h in range(2):
                ref[8 * j + 2 * i + h] = value[16 * h:16 * h + 16, 128 * i:128 * i + 128]

    def natural(src, dst):
        n = src.shape[0] // 4
        for i in range(4):
            block = jnp.concatenate([src[n * i + j] for j in range(n)], axis=0).astype(F32)
            dst[128 * i:128 * i + 128] = block.T.astype(BF16)

    mine = parent[0]
    own_grand = [jnp.where(mine == g, 1.0, 0.0).astype(F32) for g in range(4)]
    own_child = [own_grand[0] + own_grand[1], own_grand[2] + own_grand[3]]
    slot = lax.broadcasted_iota(jnp.int32, (16, 128), 0)
    picks = jnp.zeros((16, 128), F32)
    for g in range(4):
        picks = picks + jnp.where(slot == g, own_grand[g], 0.0)
    weight[l] = picks.astype(BF16)
    share = pl.ds(pl.multiple_of(l * 16, 16), 16)

    pl.semaphore_wait(barrier, PANEL - 1 + 5)
    loads[9].wait()

    def first_rounds():
        for there in (z_peers[1], z_peers[7]):
            signal(round_sem.at[0], there, p)
        loads[1].start()
        loads[0].wait()
        lower_mask(inverse, inverse, p * 256, 0, 32)
        pl.semaphore_wait(round_sem.at[0], 2)
        for there in (z_peers[2], z_peers[6]):
            signal(round_sem.at[1], there, p)

    gather_panel(0, "SIDES", sides_all, first_rounds)
    solved_all[p] = dot(inverse[...], flat(sides_all)).astype(BF16)

    def last_round():
        pl.semaphore_wait(round_sem.at[1], 2)
        for there in x_peers:
            signal(round_sem.at[2], there, p)
        for copy in loads[2:8]:
            copy.start()
        loads[1].wait()
        loads[2].wait()
        lower_mask(grand, grand, m8 * 512, p * 512, 64)

    gather_panel(1, "SOLVED", solved_all, last_round)
    pl.semaphore_wait(round_sem.at[2], 3)

    loads[8].wait()
    loads[10].wait()

    def update(k, t):
        keep = tiles[k, 0, p * 4 + t].astype(F32)
        return dot(panels[k, t * 128:(t + 1) * 128, :], flat(solved_all)) * keep

    for step in range(4):
        t = lax.rem(l // 8 + 1 + step, 4)
        keep = tiles[0, 0, p * 4 + t].astype(F32)
        rows = pl.ds(pl.multiple_of(t * 128, 128), 128)
        value = dot(panels[0, rows, :], flat(solved_all)) * keep
        u0_out[pl.ds(t * 8, 8)] = value.astype(BF16).reshape(8, 16, 128)

        def give(k, c):
            there = t * 8 + lax.rem(m8 + k, 8)

            @pl.when(there != l)
            def _():
                send("U0", u0_out.at[there], u0_in.at[l], (there, p))

            return c

        lax.fori_loop(0, 8, give, 0)
    u0_in[l] = u0_out[l]
    to_leaf("WEIGHT", LEAF, 0, l, lambda q: weight.at[l], weight.at[l])
    loads[3].wait()
    lower_mask(child_all.at[y], child_all.at[y], m16 * 256, p * 512, 64)
    loads[4].wait()
    lower_mask(root.at[y], root.at[y], l * 128, p * 512, 64)
    to_chips("CHILD", child_all.at[y], child_all.at[y])

    to_chips("RLINE", root.at[y], root.at[y])
    for t in range(4):
        at = slice(t * 128, (t + 1) * 128)
        u1_part[at] = update(1, t)
        u2_part[at] = update(2, t)
    u2_part[share] = u2_part[share] - tops[6].astype(F32)
    for c in range(2):
        work[...] = u1_part[...] * own_child[c]
        work[share] = work[share] - tops[4 + c].astype(F32)

        def store(j, v):
            ctop_out[16 * c + j] = v

        cut(work[...].T, store)
    ctop[l] = ctop_out[l]
    arrived("WEIGHT", weight.at[pl.ds(0, LEAF - 1)])
    arrived("U0", u0_in.at[pl.ds(0, LEAF - 1)])

    def collect(d, sums):
        w = weight[d].astype(F32)
        u = u0_in[d].astype(F32)
        return tuple(s - w[g:g + 1, :] * u for g, s in enumerate(sums))

    sums = lax.fori_loop(0, LEAF, collect, tuple(tops[g].astype(F32) for g in range(4)), unroll=4)
    for g in range(4):
        gright_out[g] = sums[g].astype(BF16)
    gright[l] = gright_out[l // 8]
    to_leaf("GRIGHT", LEAF, 0, l, lambda q: gright_out.at[q // 8], gright.at[l])
    to_leaf("CTOP", LEAF, 0, l, lambda q: ctop_out.at[q], ctop.at[l])
    arrived("GRIGHT", gright.at[pl.ds(0, LEAF - 1)])
    scattered(dot(grand[...], flat(gright)), gred_out)
    gred[p] = gred_out[p]
    to_panel("GRED", lambda q: gred_out.at[q], gred.at[p])
    arrived("CTOP", ctop.at[pl.ds(0, LEAF - 1)])
    cpiece[...] = total(ctop)
    arrived("GRED", gred.at[pl.ds(0, PANEL - 1)])
    gsol[p] = total(gred).astype(BF16)
    to_panel("GSOL", lambda q: gsol.at[p], gsol.at[p])
    for i in range(5, 8):
        loads[i].wait()
    arrived("GSOL", gsol.at[pl.ds(0, PANEL - 1)])

    def store(j, v):
        cred_out[j] = v

    cut(dot(cp[...], flat(gsol)).T, store)
    cred[m16] = cred_out[m16]
    to_leaf("CRED", 16, l16, m16, lambda q: cred_out.at[q], cred.at[m16])
    to_chips("RC", rc_all.at[y], rc_all.at[y])

    back = (dot(rg[...], flat(gsol)) + u2_part[...]).T.astype(BF16)
    for j in range(4):
        for i in range(4):
            for h in range(2):
                at = 32 * j + 16 * h
                rtop_out[8 * j + 2 * i + h] = back[at:at + 16, 128 * i:128 * i + 128]

    arrived("CRED", cred.at[pl.ds(0, 15)])
    cres_piece[0] = (-(cpiece[...] + total(cred))).astype(BF16)
    to_line("CRIGHT", 16, l16, m16, cres_piece.at[0], cright.at[4 * y + own_i], 2 * own_y + core)

    @pl.when(diag)
    def _():
        cright[4 * y + own_i] = cres_piece[0]

    def to_rtop(k, c):
        j = lax.rem(k, 4)
        there = 8 * y + k // 4
        q = 2 * j + core

        @pl.when(jnp.logical_or(there != l, q != p))
        def _():
            send("RTOP", rtop_out.at[8 * j + k // 4], rtop.at[l], (there, q))

        return c

    lax.fori_loop(0, 32, to_rtop, 0)

    @pl.when(root_diag)
    def _():
        rtop[l] = rtop_out[l]

    arrived("CHILD", child_all.at[pl.ds(0, 3)])
    arrived_but_self("CRIGHT", cright, diag, 16)

    def summed(x, value, out, inbox):
        out[...] = value.astype(BF16)
        to_sibling(x, out, inbox)
        arrived(x, inbox)
        return out[...].astype(F32) + inbox[...].astype(F32)

    cs[...] = summed("CSIB", sum(dot_nt(strip(cright, j), child_all[j]) for j in range(4)), cs_out, cs_in).astype(BF16)
    arrived("RC", rc_all.at[pl.ds(0, 3)])

    for j in range(4):
        put_strip2(rred_out, j, dot_nt(cs[...], rc_all[j]))
    rred[l] = rred_out[l]
    to_leaf("RRED", LEAF, 0, l, lambda q: rred_out.at[q], rred.at[l])
    for n in range(8):
        at = slice(n * 256, (n + 1) * 256)
        inverse_t[at, :] = inverse[:, at].T
    arrived_but_self("RTOP", rtop, root_diag, 32)
    root_top = total(rtop)
    arrived("RLINE", root.at[pl.ds(0, 3)])
    arrived("RRED", rred.at[pl.ds(0, LEAF - 1)])
    rright[l] = (-(root_top + total(rred))).astype(BF16)
    to_leaf("RRIGHT", LEAF, 0, l, lambda q: rright.at[l], rright.at[l])
    for n in range(8):
        at = slice(n * 256, (n + 1) * 256)
        panel_t[at, :] = panels[0, :, at].T
    arrived("RRIGHT", rright.at[pl.ds(0, LEAF - 1)])
    rs[...] = summed("RSIB", sum(dot_nt(strip2(rright, j), root[j]) for j in range(4)), rs_out, rs_in).astype(BF16)
    for j in range(4):
        put_strip2(rback_out, j, dot(rs[...], root[j]))
    rback[l] = rback_out[l]
    to_leaf("RBACK", LEAF, 0, l, lambda q: rback_out.at[q], rback.at[l])
    arrived("RBACK", rback.at[pl.ds(0, LEAF - 1)])
    rres[l] = total(rback).astype(BF16)
    to_leaf("RRES", LEAF, 0, l, lambda q: rres.at[l], rres.at[l])
    rnat_at = 8 * root_i + 2 * y + root_half
    to_line("RNAT", LEAF, 0, l, rres.at[l], rnat.at[rnat_at], 2 * root_y + core)

    @pl.when(root_diag)
    def _():
        rnat[rnat_at] = rres[l]

    arrived("RRES", rres.at[pl.ds(0, LEAF - 1)])

    crs = summed("CRSIB", sum(dot(strip2(rres, j), rc_all[j]) for j in range(4)), cr_out, cr_in)
    residual_c = (cs[...].astype(F32) - crs).astype(BF16)
    for j in range(4):
        put_strip(cback_out, j, dot(residual_c, child_all[j]))
    cback[m16] = cback_out[m16]
    to_leaf("CBACK", 16, l16, m16, lambda q: cback_out.at[q], cback.at[m16])

    def masked(k, value):
        for t in range(4):
            keep = tiles[k, 0, p * 4 + t].astype(F32)
            ancestor[t * 128:(t + 1) * 128] = (value[t * 128:(t + 1) * 128] * keep).astype(BF16)

    def pull_from(k, first):
        for n in range(8):
            at = slice(n * 256, (n + 1) * 256)
            value = dot_t(panels[k, :, at], ancestor[...])
            pulled[at, :] = value if first else pulled[at, :] + value

    arrived_but_self("RNAT", rnat, root_diag, 32)
    natural(rnat, root_nat)
    gb_part[...] = dot_t(rg[...], root_nat[...])
    arrived("CBACK", cback.at[pl.ds(0, 15)])
    cres_piece[1] = total(cback).astype(BF16)
    to_line("CRES", 16, l16, m16, cres_piece.at[1], cnat.at[4 * own_i + y], 2 * own_y + core)
    to_line("CFAR", 16, 16 - l16, m16, cres_piece.at[1], cfar.at[4 * own_i + y], 2 * own_y + core)

    @pl.when(diag)
    def _():
        cnat[4 * own_i + y] = cres_piece[1]

    top_out[6] = root_nat[share]
    masked(2, root_nat[...].astype(F32))
    pull_from(2, True)
    arrived_but_self("CRES", cnat, diag, 16)
    natural(cnat, child_nat)

    scattered(dot_t(cp[...], child_nat[...]) + gb_part[...], gback_out)
    gback[p] = gback_out[p]
    to_panel("GBACK", lambda q: gback_out.at[q], gback.at[p])
    arrived("CFAR", cfar)
    natural(cfar, far_nat)
    arrived("GBACK", gback.at[pl.ds(0, PANEL - 1)])
    gresid[p] = (gsol[p].astype(F32) - total(gback)).astype(BF16)
    to_panel("GRESID", lambda q: gresid.at[p], gresid.at[p])
    near = jnp.where(l < 16, 1.0, 0.0).astype(F32)
    here = child_nat[share].astype(F32)
    there = far_nat[share].astype(F32)
    top_out[4] = (here * near + there * (1.0 - near)).astype(BF16)
    top_out[5] = (there * near + here * (1.0 - near)).astype(BF16)
    from_near = own_child[0] * near + own_child[1] * (1.0 - near)
    masked(1, child_nat[...].astype(F32) * from_near + far_nat[...].astype(F32) * (1.0 - from_near))
    arrived("GRESID", gresid.at[pl.ds(0, PANEL - 1)])
    scattered(dot_t(grand[...], flat(gresid)), gback2_out)
    gback2[m8] = gback2_out[m8]
    to_leaf("GBACK2", 8, l8, m8, lambda q: gback2_out.at[q], gback2.at[m8])
    pull_from(1, False)
    arrived("GBACK2", gback2.at[pl.ds(0, 7)])
    gres[l] = total(gback2).astype(BF16)
    order = (4, 3, 5, 2, 6, 1, 7)
    for k in order:
        pltpu.make_async_remote_copy(
            gres.at[l], gres.at[l], z_send_sem, z_sem.at[k], device_id=(z_peers[k], p), device_id_type=MESH
        ).start()
    for there in x_peers:
        send("GRES", gres.at[l], gres.at[l], (there, p))
    for k in order[::-1]:
        came = z_peers[8 - k]
        pltpu.make_async_copy(gres.at[came], gres.at[came], z_sem.at[k]).wait()
        for there in x_peers:
            send("GRES", gres.at[came], gres.at[came], (there, p))
    arrived("GRES", gres.at[pl.ds(0, 24)])

    def grand_of(g):
        return gres[g * 8:(g + 1) * 8].reshape(512, 128).astype(F32)

    masked(0, sum(grand_of(g) * own_grand[g] for g in range(4)))
    at64 = pl.ds(pl.multiple_of(lax.rem(l, 4) * 16, 16), 16)
    panel_order = (4, 5, 3, 2, 6, 7, 1, 0)
    for k in panel_order:
        q = lax.rem(p + k, PANEL)
        rows = pl.ds(pl.multiple_of(q * 256, 256), 256)
        pull_out[q] = (pulled[rows, :] + dot(panel_t[rows, :], ancestor[...])).astype(BF16)
        if k:
            send("PULL", pull_out.at[q], pull.at[p], (l, q))
    pull[p] = pull_out[p]
    for g in range(4):
        top_out[g] = gres[g * 8 + l // 4, at64]
    arrived("PULL", pull.at[pl.ds(0, PANEL - 1)])
    residual = (solved_all[p].astype(F32) - total(pull)).astype(BF16)
    for k in panel_order:
        q = lax.rem(p + k, PANEL)
        rows = pl.ds(pl.multiple_of(q * 256, 256), 256)
        leafo_out[q] = dot(inverse_t[rows, :], residual).astype(BF16)
        if k:
            send("OUT", leafo_out.at[q], leafo.at[p], (l, q))
    leafo[p] = leafo_out[p]
    arrived("OUT", leafo.at[pl.ds(0, PANEL - 1)])
    leaf_out[...] = total(leafo).astype(BF16)

    def sent(x, ref):
        pltpu.make_async_copy(ref, ref, send_sem.at[X[x]]).wait()

    for x, ref, n in [
        ("SIDES", sides_all, 3), ("SIDES_PAIR", sides_all, 4), ("SOLVED_PAIR", solved_all, 4), ("WEIGHT", weight, 31), ("SOLVED", solved_all, 3), ("U0", u0_in, 31), ("GRIGHT", gright, 31),
        ("GRED", gred, 7), ("GSOL", gsol, 7), ("CHILD", child_all, 3), ("RC", rc_all, 3), ("RLINE", root, 3), ("CTOP", ctop, 31), ("CRED", cred, 15),
        ("RRED", rred, 31), ("RRIGHT", rright, 31), ("RBACK", rback, 31), ("RRES", rres, 31), ("CBACK", cback, 15),
        ("CFAR", cfar, 16), ("GBACK", gback, 7), ("GRESID", gresid, 7), ("GBACK2", gback2, 7), ("GRES", gres, 24),
        ("PULL", pull, 7), ("OUT", leafo, 7),
    ]:
        sent(x, ref.at[pl.ds(0, n)])
    pltpu.make_async_copy(gres.at[pl.ds(0, 7)], gres.at[pl.ds(0, 7)], z_send_sem).wait()
    for x, ref in [("CSIB", cs_in), ("RSIB", rs_in), ("CRSIB", cr_in)]:
        sent(x, ref)

    @pl.when(diag)
    def _():
        for x, ref, n in [("CRIGHT", cright, 15), ("CRES", cnat, 15)]:
            sent(x, ref.at[pl.ds(0, n)])

    @pl.when(jnp.logical_not(diag))
    def _():
        for x, ref in [("CRIGHT", cright), ("CRES", cnat)]:
            sent(x, ref)

    @pl.when(root_diag)
    def _():
        for x, ref in [("RTOP", rtop), ("RNAT", rnat)]:
            sent(x, ref.at[pl.ds(0, 31)])

    @pl.when(jnp.logical_not(root_diag))
    def _():
        for x, ref in [("RTOP", rtop), ("RNAT", rnat)]:
            sent(x, ref)


def per_device(
    leaf_sides, leaf_inverse, leaf_panels, parent_map, tile_mask, top_sides,
    grand_inverse, child_inverse, root_inverse, child_panels, root_grand, root_child,
):
    def bf(*shape):
        return pltpu.VMEM(shape, BF16)

    def pieces(n, rows):
        return bf(n, rows, 128)

    vmem = pl.BlockSpec(memory_space=pltpu.VMEM)
    smem = pl.BlockSpec(memory_space=pltpu.SMEM)
    hbm = pl.BlockSpec(memory_space=pltpu.HBM)
    def f32(*shape):
        return pltpu.VMEM(shape, F32)

    sems = pltpu.SemaphoreType.DMA((len(X),))
    scratch = [
        bf(256, 2048), bf(3, 512, 2048), bf(512, 512), bf(4, 256, 512), bf(4, 128, 512),
        bf(512, 512), bf(512, 512), bf(4, 512, 256), pltpu.SemaphoreType.DMA((11,)), sems, sems,
        pltpu.SemaphoreType.DMA((2, 4)), pltpu.SemaphoreType.DMA((8,)), pltpu.SemaphoreType.DMA, pltpu.SemaphoreType.REGULAR((3,)),
        pieces(8, 256), bf(7, 16, 128), pltpu.SMEM((3, 1, 32), jnp.int32), pieces(32, 16), pieces(8, 256), pieces(32, 16), pieces(32, 16),
        f32(512, 128), f32(512, 128), f32(512, 128),
        pieces(4, 16), pieces(32, 16), pieces(8, 64), pieces(8, 64), pieces(8, 64),
        pieces(32, 32), pieces(32, 32), pieces(16, 32), pieces(16, 32),
        f32(32, 128), pieces(16, 32), bf(32, 256), bf(32, 256), bf(32, 256),
        pieces(32, 16), pieces(32, 16), pieces(32, 16), pieces(32, 16), pieces(32, 16),
        bf(32, 128), bf(32, 128), bf(32, 128), pieces(32, 16), pieces(32, 16), pieces(32, 16),
        pieces(32, 16), bf(32, 256), bf(32, 256),
        pieces(16, 32), pieces(16, 32), pieces(2, 32), pieces(16, 32), pieces(16, 32),
        pieces(8, 64), pieces(8, 64), pieces(8, 64),
        pieces(8, 64), pieces(8, 64), pieces(32, 64),
        f32(2048, 128), pieces(8, 256), pieces(8, 256), pieces(8, 256), pieces(8, 256),
        bf(512, 128), f32(512, 128), bf(2048, 256), bf(2048, 512), bf(512, 128), bf(512, 128), bf(512, 128),
    ]
    return pl.pallas_call(
        kernel,
        out_shape=(jax.ShapeDtypeStruct((256, 128), BF16), jax.ShapeDtypeStruct((7, 16, 128), BF16)),
        in_specs=[smem, hbm, hbm, hbm, hbm, hbm, hbm, hbm, hbm, hbm, hbm, hbm],
        out_specs=(vmem, vmem),
        scratch_shapes=scratch,
        compiler_params=pltpu.CompilerParams(collective_id=0, has_side_effects=True, vmem_limit_bytes=VMEM_BYTES),
        cost_estimate=pl.CostEstimate(flops=2_400_000_000, bytes_accessed=12_000_000, transcendentals=0),
        name="solve",
    )(
        parent_map, tile_mask.transpose(1, 0, 2), leaf_sides, leaf_inverse, leaf_panels, top_sides,
        grand_inverse, child_inverse, root_inverse, child_panels, root_grand, root_child,
    )


def solution(mesh):
    placed = (
        P(("leaf", "panel"), None),
        P(("leaf", "panel"), None),
        P(None, "panel", "leaf"),
        P("leaf"),
        P("leaf", None, None),
        P(None, ("panel", "leaf"), None),
        P("leaf", "panel"),
        P("leaf", "panel"),
        P("leaf", "panel"),
        P("panel", "leaf"),
        P("panel", "leaf"),
        P("panel", "leaf"),
    )
    return jax.shard_map(
        per_device,
        mesh=mesh,
        in_specs=placed,
        out_specs=(P(("leaf", "panel"), None), P(None, ("panel", "leaf"), None)),
        check_vma=False,
    )
```

```python
import functools

import jax
import jax.numpy as jnp
from jax import lax
from jax.experimental import pallas as pl
from jax.experimental.pallas import tpu as pltpu
from jax.sharding import PartitionSpec as P

MESH = pl.DeviceIdType.MESH
F32 = jnp.float32
BF16 = jnp.bfloat16
LEAF = 32
PANEL = 8
VMEM_BYTES = 60 << 20

NAMES = (
    "SIDES", "SIDES_PAIR", "WEIGHT", "SOLVED", "SOLVED_PAIR", "U0", "GRIGHT", "GRED", "GSOL", "CHILD", "RC", "RLINE", "CTOP",
    "CRED", "CRIGHT", "CSIB", "RTOP", "RRED", "RRIGHT", "RSIB", "RBACK", "RRES", "RNAT", "CRSIB", "CBACK", "CRES", "CFAR",
    "GBACK", "GRESID", "GBACK2", "GRES", "PULL", "OUT",
)
X = {name: i for i, name in enumerate(NAMES)}


def lower_mask(ref, out, row0, col0, tile):
    rows, cols = ref.shape

    def body(i, c):
        at = pl.ds(pl.multiple_of(i * tile, tile), tile)
        row = row0 + i * tile + lax.broadcasted_iota(jnp.int32, (tile, cols), 0)
        col = col0 + lax.broadcasted_iota(jnp.int32, (tile, cols), 1)
        out[at, :] = jnp.where(row >= col, ref[at, :].astype(F32), 0.0).astype(BF16)
        return c

    lax.fori_loop(0, rows // tile, body, 0)


def dot(a, b):
    return jnp.dot(a, b, preferred_element_type=F32)


def dot_t(a, b):
    return lax.dot_general(a, b, (((0,), (0,)), ((), ())), preferred_element_type=F32)


def dot_nt(a, b):
    return lax.dot_general(a, b, (((1,), (1,)), ((), ())), preferred_element_type=F32)


def kernel(
    parent, tiles_h, sides_h, inverse_h, panels_h, tops_h, grand_h, child_h, root_h, cp_h, rg_h, rc_h,
    leaf_out, top_out,
    inverse, panels, grand, child_all, root, cp, rg, rc_all,
    in_sem, send_sem, recv_sem, pair_sem, z_sem, z_send_sem, round_sem,
    sides_all, tops, tiles, weight, solved_all, u0_out, u0_in, u1_part, u2_part, work,
    gright_out, gright, gred_out, gred, gsol, ctop_out, ctop, cred_out, cred, cpiece, cright, cs_out, cs_in, cs,
    rtop_out, rtop, rred_out, rred, rright, rs_out, rs_in, rs, rback_out, rback, rres, rnat, cr_out, cr_in,
    cback_out, cback, cres_piece, cnat, cfar, gback_out, gback, gresid, gback2_out, gback2, gres,
    pulled, pull_out, pull, leafo_out, leafo, ancestor, gb_part, inverse_t, panel_t, root_nat, child_nat, far_nat,
):
    l = lax.axis_index("leaf")
    p = lax.axis_index("panel")
    l8, l16 = l // 8 * 8, l // 16 * 16
    m8, m16 = l - l8, l - l16
    y = p // 2
    core = p - 2 * y
    own_y = m16 // 4
    own_i = m16 - 4 * own_y
    diag = own_y == y
    root_y = l // 8
    root_i = (l - 8 * root_y) // 2
    root_half = l - l // 2 * 2
    root_diag = root_y == y

    loads = []
    for i, (src, dst) in enumerate(
        [(inverse_h, inverse), (panels_h, panels), (grand_h, grand), (child_h, child_all.at[y]), (root_h, root.at[y]), (cp_h, cp), (rg_h, rg), (rc_h, rc_all.at[y]), (tops_h, tops), (sides_h, sides_all.at[p]), (tiles_h, tiles)]
    ):
        loads.append(pltpu.make_async_copy(src, dst, in_sem.at[i]))
    loads[9].start()
    loads[0].start()
    loads[8].start()
    loads[10].start()

    barrier = pltpu.get_barrier_semaphore()

    x_of = lax.rem(l, 4)
    x_peers = [l - x_of + lax.rem(x_of + k, 4) for k in range(1, 4)]
    z_peers = {k: lax.rem(l + 4 * k, LEAF) for k in range(1, 8)}

    def signal(semaphore, leaf, panel):
        pl.semaphore_signal(semaphore, inc=1, device_id=(leaf, panel), device_id_type=MESH)

    for k in range(1, PANEL):
        signal(barrier, l, lax.rem(p + k, PANEL))
    for there in x_peers + [z_peers[1], z_peers[7]]:
        signal(barrier, there, p)

    def send(x, src, dst, device):
        pltpu.make_async_remote_copy(src, dst, send_sem.at[X[x]], recv_sem.at[X[x]], device_id=device, device_id_type=MESH).start()

    def arrived(x, ref):
        pltpu.make_async_copy(ref, ref, recv_sem.at[X[x]]).wait()

    def to_panel(x, src_of, dst):
        def body(k, c):
            q = lax.rem(p + k, PANEL)
            send(x, src_of(q), dst, (l, q))
            return c

        lax.fori_loop(1, PANEL, body, 0)

    def to_leaf(x, n, base, me, src_of, dst):
        def body(k, c):
            q = lax.rem(me + k, n)
            send(x, src_of(q), dst, (base + q, p))
            return c

        lax.fori_loop(n // 2, n, body, 0)
        lax.fori_loop(1, n // 2, body, 0)

    def total(ref):
        return jnp.sum(ref[...].astype(F32), axis=0)

    def flat(ref):
        return ref[...].reshape(ref.shape[0] * ref.shape[1], ref.shape[2])

    def scattered(value, out):
        out[...] = value.astype(BF16).reshape(out.shape)

    def arrived_but_self(x, ref, has_self, n):
        @pl.when(has_self)
        def _():
            arrived(x, ref.at[pl.ds(0, n - 1)])

        @pl.when(jnp.logical_not(has_self))
        def _():
            arrived(x, ref.at[pl.ds(0, n)])

    def to_line(x, n, base, me, src, dst, q):
        def body(k, c):
            there = base + lax.rem(me + k, n)

            @pl.when(jnp.logical_or(there != l, q != p))
            def _():
                send(x, src, dst, (there, q))

            return c

        lax.fori_loop(n // 2, n, body, 0)
        lax.fori_loop(0, n // 2, body, 0)

    def to_sibling(x, src, dst):
        send(x, src, dst, (l, p + 1 - 2 * core))

    def to_chips(x, src, dst):
        def body(k, c):
            send(x, src, dst, (l, lax.rem(p + 2 * k, PANEL)))
            return c

        lax.fori_loop(1, 4, body, 0)

    def gather_panel(which, x, ref, beside):
        to_chips_each(which, x, ref)
        to_sibling(x + "_PAIR", ref.at[p], ref.at[p])
        beside()
        for k in range(1, 4):
            came = lax.rem(p + PANEL - 2 * k, PANEL)
            pltpu.make_async_copy(ref.at[came], ref.at[came], pair_sem.at[which, k]).wait()
            to_sibling(x + "_PAIR", ref.at[came], ref.at[came])
        arrived(x + "_PAIR", ref.at[pl.ds(0, 4)])

    def to_chips_each(which, x, ref):
        for k in range(1, 4):
            pltpu.make_async_remote_copy(
                ref.at[p], ref.at[p], send_sem.at[X[x]], pair_sem.at[which, k],
                device_id=(l, lax.rem(p + 2 * k, PANEL)), device_id_type=MESH,
            ).start()

    def cut(value, store):
        value = value.astype(BF16)
        for j in range(4):
            for i in range(4):
                store(4 * j + i, value[32 * j:32 * j + 32, 128 * i:128 * i + 128])

    def strip(ref, j):
        return jnp.concatenate([ref[4 * j + i] for i in range(4)], axis=1)

    def put_strip(ref, j, value):
        value = value.astype(BF16)
        for i in range(4):
            ref[4 * j + i] = value[:, 128 * i:128 * i + 128]

    def strip2(ref, j):
        return jnp.concatenate(
            [jnp.concatenate([ref[8 * j + 2 * i], ref[8 * j + 2 * i + 1]], axis=0) for i in range(4)], axis=1
        )

    def put_strip2(ref, j, value):
        value = value.astype(BF16)
        for i in range(4):
            for h in range(2):
                ref[8 * j + 2 * i + h] = value[16 * h:16 * h + 16, 128 * i:128 * i + 128]

    def natural(src, dst):
        n = src.shape[0] // 4
        for i in range(4):
            block = jnp.concatenate([src[n * i + j] for j in range(n)], axis=0).astype(F32)
            dst[128 * i:128 * i + 128] = block.T.astype(BF16)

    mine = parent[0]
    own_grand = [jnp.where(mine == g, 1.0, 0.0).astype(F32) for g in range(4)]
    own_child = [own_grand[0] + own_grand[1], own_grand[2] + own_grand[3]]
    slot = lax.broadcasted_iota(jnp.int32, (16, 128), 0)
    picks = jnp.zeros((16, 128), F32)
    for g in range(4):
        picks = picks + jnp.where(slot == g, own_grand[g], 0.0)
    weight[l] = picks.astype(BF16)
    share = pl.ds(pl.multiple_of(l * 16, 16), 16)

    pl.semaphore_wait(barrier, PANEL - 1 + 5)
    loads[9].wait()

    def first_rounds():
        for there in (z_peers[1], z_peers[7]):
            signal(round_sem.at[0], there, p)
        loads[1].start()
        loads[0].wait()
        lower_mask(inverse, inverse, p * 256, 0, 32)
        pl.semaphore_wait(round_sem.at[0], 2)
        for there in (z_peers[2], z_peers[6]):
            signal(round_sem.at[1], there, p)

    gather_panel(0, "SIDES", sides_all, first_rounds)
    solved_all[p] = dot(inverse[...], flat(sides_all)).astype(BF16)

    def last_round():
        pl.semaphore_wait(round_sem.at[1], 2)
        for there in x_peers:
            signal(round_sem.at[2], there, p)
        for copy in loads[2:8]:
            copy.start()
        loads[1].wait()
        loads[2].wait()
        lower_mask(grand, grand, m8 * 512, p * 512, 64)

    gather_panel(1, "SOLVED", solved_all, last_round)
    pl.semaphore_wait(round_sem.at[2], 3)

    loads[8].wait()
    loads[10].wait()

    def update(k, t):
        keep = tiles[k, 0, p * 4 + t].astype(F32)
        return dot(panels[k, t * 128:(t + 1) * 128, :], flat(solved_all)) * keep

    for step in range(4):
        t = lax.rem(l // 8 + 1 + step, 4)
        keep = tiles[0, 0, p * 4 + t].astype(F32)
        rows = pl.ds(pl.multiple_of(t * 128, 128), 128)
        value = dot(panels[0, rows, :], flat(solved_all)) * keep
        u0_out[pl.ds(t * 8, 8)] = value.astype(BF16).reshape(8, 16, 128)

        def give(k, c):
            there = t * 8 + lax.rem(m8 + k, 8)

            @pl.when(there != l)
            def _():
                send("U0", u0_out.at[there], u0_in.at[l], (there, p))

            return c

        lax.fori_loop(0, 8, give, 0)
    u0_in[l] = u0_out[l]
    to_leaf("WEIGHT", LEAF, 0, l, lambda q: weight.at[l], weight.at[l])
    loads[3].wait()
    lower_mask(child_all.at[y], child_all.at[y], m16 * 256, p * 512, 64)
    loads[4].wait()
    lower_mask(root.at[y], root.at[y], l * 128, p * 512, 64)
    to_chips("CHILD", child_all.at[y], child_all.at[y])

    to_chips("RLINE", root.at[y], root.at[y])
    for t in range(4):
        at = slice(t * 128, (t + 1) * 128)
        u1_part[at] = update(1, t)
        u2_part[at] = update(2, t)
    u2_part[share] = u2_part[share] - tops[6].astype(F32)
    for c in range(2):
        work[...] = u1_part[...] * own_child[c]
        work[share] = work[share] - tops[4 + c].astype(F32)

        def store(j, v):
            ctop_out[16 * c + j] = v

        cut(work[...].T, store)
    ctop[l] = ctop_out[l]
    arrived("WEIGHT", weight.at[pl.ds(0, LEAF - 1)])
    arrived("U0", u0_in.at[pl.ds(0, LEAF - 1)])

    def collect(d, sums):
        w = weight[d].astype(F32)
        u = u0_in[d].astype(F32)
        return tuple(s - w[g:g + 1, :] * u for g, s in enumerate(sums))

    sums = lax.fori_loop(0, LEAF, collect, tuple(tops[g].astype(F32) for g in range(4)), unroll=4)
    for g in range(4):
        gright_out[g] = sums[g].astype(BF16)
    gright[l] = gright_out[l // 8]
    to_leaf("GRIGHT", LEAF, 0, l, lambda q: gright_out.at[q // 8], gright.at[l])
    to_leaf("CTOP", LEAF, 0, l, lambda q: ctop_out.at[q], ctop.at[l])
    arrived("GRIGHT", gright.at[pl.ds(0, LEAF - 1)])
    scattered(dot(grand[...], flat(gright)), gred_out)
    gred[p] = gred_out[p]
    to_panel("GRED", lambda q: gred_out.at[q], gred.at[p])
    arrived("CTOP", ctop.at[pl.ds(0, LEAF - 1)])
    cpiece[...] = total(ctop)
    arrived("GRED", gred.at[pl.ds(0, PANEL - 1)])
    gsol[p] = total(gred).astype(BF16)
    to_panel("GSOL", lambda q: gsol.at[p], gsol.at[p])
    for i in range(5, 8):
        loads[i].wait()
    arrived("GSOL", gsol.at[pl.ds(0, PANEL - 1)])

    def store(j, v):
        cred_out[j] = v

    cut(dot(cp[...], flat(gsol)).T, store)
    cred[m16] = cred_out[m16]
    to_leaf("CRED", 16, l16, m16, lambda q: cred_out.at[q], cred.at[m16])
    to_chips("RC", rc_all.at[y], rc_all.at[y])

    back = (dot(rg[...], flat(gsol)) + u2_part[...]).T.astype(BF16)
    for j in range(4):
        for i in range(4):
            for h in range(2):
                at = 32 * j + 16 * h
                rtop_out[8 * j + 2 * i + h] = back[at:at + 16, 128 * i:128 * i + 128]

    arrived("CRED", cred.at[pl.ds(0, 15)])
    cres_piece[0] = (-(cpiece[...] + total(cred))).astype(BF16)
    to_line("CRIGHT", 16, l16, m16, cres_piece.at[0], cright.at[4 * y + own_i], 2 * own_y + core)

    @pl.when(diag)
    def _():
        cright[4 * y + own_i] = cres_piece[0]

    def to_rtop(k, c):
        j = lax.rem(k, 4)
        there = 8 * y + k // 4
        q = 2 * j + core

        @pl.when(jnp.logical_or(there != l, q != p))
        def _():
            send("RTOP", rtop_out.at[8 * j + k // 4], rtop.at[l], (there, q))

        return c

    lax.fori_loop(0, 32, to_rtop, 0)

    @pl.when(root_diag)
    def _():
        rtop[l] = rtop_out[l]

    arrived("CHILD", child_all.at[pl.ds(0, 3)])
    arrived_but_self("CRIGHT", cright, diag, 16)

    def summed(x, value, out, inbox):
        out[...] = value.astype(BF16)
        to_sibling(x, out, inbox)
        arrived(x, inbox)
        return out[...].astype(F32) + inbox[...].astype(F32)

    cs[...] = summed("CSIB", sum(dot_nt(strip(cright, j), child_all[j]) for j in range(4)), cs_out, cs_in).astype(BF16)
    arrived("RC", rc_all.at[pl.ds(0, 3)])

    for j in range(4):
        put_strip2(rred_out, j, dot_nt(cs[...], rc_all[j]))
    rred[l] = rred_out[l]
    to_leaf("RRED", LEAF, 0, l, lambda q: rred_out.at[q], rred.at[l])
    for n in range(8):
        at = slice(n * 256, (n + 1) * 256)
        inverse_t[at, :] = inverse[:, at].T
    arrived_but_self("RTOP", rtop, root_diag, 32)
    root_top = total(rtop)
    arrived("RLINE", root.at[pl.ds(0, 3)])
    arrived("RRED", rred.at[pl.ds(0, LEAF - 1)])
    rright[l] = (-(root_top + total(rred))).astype(BF16)
    to_leaf("RRIGHT", LEAF, 0, l, lambda q: rright.at[l], rright.at[l])
    for n in range(8):
        at = slice(n * 256, (n + 1) * 256)
        panel_t[at, :] = panels[0, :, at].T
    arrived("RRIGHT", rright.at[pl.ds(0, LEAF - 1)])
    rs[...] = summed("RSIB", sum(dot_nt(strip2(rright, j), root[j]) for j in range(4)), rs_out, rs_in).astype(BF16)
    for j in range(4):
        put_strip2(rback_out, j, dot(rs[...], root[j]))
    rback[l] = rback_out[l]
    to_leaf("RBACK", LEAF, 0, l, lambda q: rback_out.at[q], rback.at[l])
    arrived("RBACK", rback.at[pl.ds(0, LEAF - 1)])
    rres[l] = total(rback).astype(BF16)
    to_leaf("RRES", LEAF, 0, l, lambda q: rres.at[l], rres.at[l])
    rnat_at = 8 * root_i + 2 * y + root_half
    to_line("RNAT", LEAF, 0, l, rres.at[l], rnat.at[rnat_at], 2 * root_y + core)

    @pl.when(root_diag)
    def _():
        rnat[rnat_at] = rres[l]

    arrived("RRES", rres.at[pl.ds(0, LEAF - 1)])

    crs = summed("CRSIB", sum(dot(strip2(rres, j), rc_all[j]) for j in range(4)), cr_out, cr_in)
    residual_c = (cs[...].astype(F32) - crs).astype(BF16)
    for j in range(4):
        put_strip(cback_out, j, dot(residual_c, child_all[j]))
    cback[m16] = cback_out[m16]
    to_leaf("CBACK", 16, l16, m16, lambda q: cback_out.at[q], cback.at[m16])

    def masked(k, value):
        for t in range(4):
            keep = tiles[k, 0, p * 4 + t].astype(F32)
            ancestor[t * 128:(t + 1) * 128] = (value[t * 128:(t + 1) * 128] * keep).astype(BF16)

    def pull_from(k, first):
        for n in range(8):
            at = slice(n * 256, (n + 1) * 256)
            value = dot_t(panels[k, :, at], ancestor[...])
            pulled[at, :] = value if first else pulled[at, :] + value

    arrived_but_self("RNAT", rnat, root_diag, 32)
    natural(rnat, root_nat)
    gb_part[...] = dot_t(rg[...], root_nat[...])
    arrived("CBACK", cback.at[pl.ds(0, 15)])
    cres_piece[1] = total(cback).astype(BF16)
    to_line("CRES", 16, l16, m16, cres_piece.at[1], cnat.at[4 * own_i + y], 2 * own_y + core)
    to_line("CFAR", 16, 16 - l16, m16, cres_piece.at[1], cfar.at[4 * own_i + y], 2 * own_y + core)

    @pl.when(diag)
    def _():
        cnat[4 * own_i + y] = cres_piece[1]

    top_out[6] = root_nat[share]
    masked(2, root_nat[...].astype(F32))
    pull_from(2, True)
    arrived_but_self("CRES", cnat, diag, 16)
    natural(cnat, child_nat)

    scattered(dot_t(cp[...], child_nat[...]) + gb_part[...], gback_out)
    gback[p] = gback_out[p]
    to_panel("GBACK", lambda q: gback_out.at[q], gback.at[p])
    arrived("CFAR", cfar)
    natural(cfar, far_nat)
    arrived("GBACK", gback.at[pl.ds(0, PANEL - 1)])
    gresid[p] = (gsol[p].astype(F32) - total(gback)).astype(BF16)
    to_panel("GRESID", lambda q: gresid.at[p], gresid.at[p])
    near = jnp.where(l < 16, 1.0, 0.0).astype(F32)
    here = child_nat[share].astype(F32)
    there = far_nat[share].astype(F32)
    top_out[4] = (here * near + there * (1.0 - near)).astype(BF16)
    top_out[5] = (there * near + here * (1.0 - near)).astype(BF16)
    from_near = own_child[0] * near + own_child[1] * (1.0 - near)
    masked(1, child_nat[...].astype(F32) * from_near + far_nat[...].astype(F32) * (1.0 - from_near))
    arrived("GRESID", gresid.at[pl.ds(0, PANEL - 1)])
    scattered(dot_t(grand[...], flat(gresid)), gback2_out)
    gback2[m8] = gback2_out[m8]
    to_leaf("GBACK2", 8, l8, m8, lambda q: gback2_out.at[q], gback2.at[m8])
    pull_from(1, False)
    arrived("GBACK2", gback2.at[pl.ds(0, 7)])
    gres[l] = total(gback2).astype(BF16)
    order = (4, 3, 5, 2, 6, 1, 7)
    for k in order:
        pltpu.make_async_remote_copy(
            gres.at[l], gres.at[l], z_send_sem, z_sem.at[k], device_id=(z_peers[k], p), device_id_type=MESH
        ).start()
    for there in x_peers:
        send("GRES", gres.at[l], gres.at[l], (there, p))
    for k in order[::-1]:
        came = z_peers[8 - k]
        pltpu.make_async_copy(gres.at[came], gres.at[came], z_sem.at[k]).wait()
        for there in x_peers:
            send("GRES", gres.at[came], gres.at[came], (there, p))
    arrived("GRES", gres.at[pl.ds(0, 24)])

    def grand_of(g):
        return gres[g * 8:(g + 1) * 8].reshape(512, 128).astype(F32)

    masked(0, sum(grand_of(g) * own_grand[g] for g in range(4)))
    at64 = pl.ds(pl.multiple_of(lax.rem(l, 4) * 16, 16), 16)
    panel_order = (4, 5, 3, 2, 6, 7, 1, 0)
    for k in panel_order:
        q = lax.rem(p + k, PANEL)
        rows = pl.ds(pl.multiple_of(q * 256, 256), 256)
        pull_out[q] = (pulled[rows, :] + dot(panel_t[rows, :], ancestor[...])).astype(BF16)
        if k:
            send("PULL", pull_out.at[q], pull.at[p], (l, q))
    pull[p] = pull_out[p]
    for g in range(4):
        top_out[g] = gres[g * 8 + l // 4, at64]
    arrived("PULL", pull.at[pl.ds(0, PANEL - 1)])
    residual = (solved_all[p].astype(F32) - total(pull)).astype(BF16)
    for k in panel_order:
        q = lax.rem(p + k, PANEL)
        rows = pl.ds(pl.multiple_of(q * 256, 256), 256)
        leafo_out[q] = dot(inverse_t[rows, :], residual).astype(BF16)
        if k:
            send("OUT", leafo_out.at[q], leafo.at[p], (l, q))
    leafo[p] = leafo_out[p]
    arrived("OUT", leafo.at[pl.ds(0, PANEL - 1)])
    leaf_out[...] = total(leafo).astype(BF16)

    def sent(x, ref):
        pltpu.make_async_copy(ref, ref, send_sem.at[X[x]]).wait()

    for x, ref, n in [
        ("SIDES", sides_all, 3), ("SIDES_PAIR", sides_all, 4), ("SOLVED_PAIR", solved_all, 4), ("WEIGHT", weight, 31), ("SOLVED", solved_all, 3), ("U0", u0_in, 31), ("GRIGHT", gright, 31),
        ("GRED", gred, 7), ("GSOL", gsol, 7), ("CHILD", child_all, 3), ("RC", rc_all, 3), ("RLINE", root, 3), ("CTOP", ctop, 31), ("CRED", cred, 15),
        ("RRED", rred, 31), ("RRIGHT", rright, 31), ("RBACK", rback, 31), ("RRES", rres, 31), ("CBACK", cback, 15),
        ("CFAR", cfar, 16), ("GBACK", gback, 7), ("GRESID", gresid, 7), ("GBACK2", gback2, 7), ("GRES", gres, 24),
        ("PULL", pull, 7), ("OUT", leafo, 7),
    ]:
        sent(x, ref.at[pl.ds(0, n)])
    pltpu.make_async_copy(gres.at[pl.ds(0, 7)], gres.at[pl.ds(0, 7)], z_send_sem).wait()
    for x, ref in [("CSIB", cs_in), ("RSIB", rs_in), ("CRSIB", cr_in)]:
        sent(x, ref)

    @pl.when(diag)
    def _():
        for x, ref, n in [("CRIGHT", cright, 15), ("CRES", cnat, 15)]:
            sent(x, ref.at[pl.ds(0, n)])

    @pl.when(jnp.logical_not(diag))
    def _():
        for x, ref in [("CRIGHT", cright), ("CRES", cnat)]:
            sent(x, ref)

    @pl.when(root_diag)
    def _():
        for x, ref in [("RTOP", rtop), ("RNAT", rnat)]:
            sent(x, ref.at[pl.ds(0, 31)])

    @pl.when(jnp.logical_not(root_diag))
    def _():
        for x, ref in [("RTOP", rtop), ("RNAT", rnat)]:
            sent(x, ref)


def per_device(
    leaf_sides, leaf_inverse, leaf_panels, parent_map, tile_mask, top_sides,
    grand_inverse, child_inverse, root_inverse, child_panels, root_grand, root_child,
):
    def bf(*shape):
        return pltpu.VMEM(shape, BF16)

    def pieces(n, rows):
        return bf(n, rows, 128)

    vmem = pl.BlockSpec(memory_space=pltpu.VMEM)
    smem = pl.BlockSpec(memory_space=pltpu.SMEM)
    hbm = pl.BlockSpec(memory_space=pltpu.HBM)
    def f32(*shape):
        return pltpu.VMEM(shape, F32)

    sems = pltpu.SemaphoreType.DMA((len(X),))
    scratch = [
        bf(256, 2048), bf(3, 512, 2048), bf(512, 512), bf(4, 256, 512), bf(4, 128, 512),
        bf(512, 512), bf(512, 512), bf(4, 512, 256), pltpu.SemaphoreType.DMA((11,)), sems, sems,
        pltpu.SemaphoreType.DMA((2, 4)), pltpu.SemaphoreType.DMA((8,)), pltpu.SemaphoreType.DMA, pltpu.SemaphoreType.REGULAR((3,)),
        pieces(8, 256), bf(7, 16, 128), pltpu.SMEM((3, 1, 32), jnp.int32), pieces(32, 16), pieces(8, 256), pieces(32, 16), pieces(32, 16),
        f32(512, 128), f32(512, 128), f32(512, 128),
        pieces(4, 16), pieces(32, 16), pieces(8, 64), pieces(8, 64), pieces(8, 64),
        pieces(32, 32), pieces(32, 32), pieces(16, 32), pieces(16, 32),
        f32(32, 128), pieces(16, 32), bf(32, 256), bf(32, 256), bf(32, 256),
        pieces(32, 16), pieces(32, 16), pieces(32, 16), pieces(32, 16), pieces(32, 16),
        bf(32, 128), bf(32, 128), bf(32, 128), pieces(32, 16), pieces(32, 16), pieces(32, 16),
        pieces(32, 16), bf(32, 256), bf(32, 256),
        pieces(16, 32), pieces(16, 32), pieces(2, 32), pieces(16, 32), pieces(16, 32),
        pieces(8, 64), pieces(8, 64), pieces(8, 64),
        pieces(8, 64), pieces(8, 64), pieces(32, 64),
        f32(2048, 128), pieces(8, 256), pieces(8, 256), pieces(8, 256), pieces(8, 256),
        bf(512, 128), f32(512, 128), bf(2048, 256), bf(2048, 512), bf(512, 128), bf(512, 128), bf(512, 128),
    ]
    return pl.pallas_call(
        kernel,
        out_shape=(jax.ShapeDtypeStruct((256, 128), BF16), jax.ShapeDtypeStruct((7, 16, 128), BF16)),
        in_specs=[smem, hbm, hbm, hbm, hbm, hbm, hbm, hbm, hbm, hbm, hbm, hbm],
        out_specs=(vmem, vmem),
        scratch_shapes=scratch,
        compiler_params=pltpu.CompilerParams(collective_id=0, has_side_effects=True, vmem_limit_bytes=VMEM_BYTES, fuse_transposed_lhs_in_matmul=True),
        cost_estimate=pl.CostEstimate(flops=2_400_000_000, bytes_accessed=12_000_000, transcendentals=0),
        name="solve",
    )(
        parent_map, tile_mask.transpose(1, 0, 2), leaf_sides, leaf_inverse, leaf_panels, top_sides,
        grand_inverse, child_inverse, root_inverse, child_panels, root_grand, root_child,
    )


def solution(mesh):
    placed = (
        P(("leaf", "panel"), None),
        P(("leaf", "panel"), None),
        P(None, "panel", "leaf"),
        P("leaf"),
        P("leaf", None, None),
        P(None, ("panel", "leaf"), None),
        P("leaf", "panel"),
        P("leaf", "panel"),
        P("leaf", "panel"),
        P("panel", "leaf"),
        P("panel", "leaf"),
        P("panel", "leaf"),
    )
    return jax.shard_map(
        per_device,
        mesh=mesh,
        in_specs=placed,
        out_specs=(P(("leaf", "panel"), None), P(None, ("panel", "leaf"), None)),
        check_vma=False,
    )
```
